512 devices in a mesh: row: 16 (over z, core), col: 32 (over x, y).
Axes of the slice: x: 4, y: 8, z: 8, core: 2. Of those that a mesh axis runs over, the one named last changes fastest.
Arguments:
- kernel: float32 [16384, 16384], P('row', 'col'), may hold values from 0 to 1.5, as said below
- targets: float32 [16384, 128], P('row'), may hold values from -6 to 6
Outputs:
- factored: float32 [16384, 16384], P('row', 'col')
- solved: float32 [16384, 128], P('row')
The draws below stay inside these ranges and needn't reach their ends.
Inputs may be any that keep to these rules, and one draw needn't show every extreme that they name: kernel is symmetric and positive definite in matrix order.
All inputs are finite; a program needn't handle non-finite values.
Results may differ from the reference program's by a relative error of at most 0.00018.
Values sent between devices are 32-bit elements; how exact they have to be, the bound alone decides.
No kernel may reach another device: no remote copies, remote signals or barrier semaphores. Data moves between devices by JAX's collectives and lax.ppermute only.
A program may use at most 64 MiB of HBM per device.

```python
import math
import jax
import jax.numpy as jnp
from jax import lax

BLOCK = 128
ROW_BLOCKS = 8
PANELS = 4
RHS = 128
ORDER = 16384
COL_BLOCKS = 4
N_ROW = 16
N_COL = 32


def draw_kernel(key, part):
    key = jax.random.fold_in(key, 7)
    order = BLOCK * ROW_BLOCKS * N_ROW
    column_blocks = order // (BLOCK * N_COL)
    points = jax.random.uniform(key, (order, 3), jnp.float32)
    noise = 0.5
    reach = (1000.0 / (8.0 * math.pi * order)) ** (1.0 / 3.0)
    squared = jnp.zeros((order, order), jnp.float32)
    for axis_pos in range(3):
        spread = points[:, axis_pos][:, None] - points[:, axis_pos][None, :]
        squared = squared + spread * spread
    matrix = jnp.exp(-jnp.sqrt(squared) / reach) + noise * jnp.eye(order, dtype=jnp.float32)
    stored = matrix.reshape(ROW_BLOCKS, N_ROW, BLOCK, column_blocks, N_COL, BLOCK).transpose(1, 0, 2, 4, 3, 5).reshape(order, order)
    return stored.astype(jnp.float32)


def steps_of(stream_key, extent, split, least, high):
    def one(axis_at, blocks):
        draws = jax.random.uniform(jax.random.fold_in(jax.random.fold_in(stream_key, 6), axis_at), (blocks,), jnp.float32, least / len(split), high / len(split))
        return jnp.repeat(jnp.exp(draws), extent[axis_at] // blocks).reshape((-1,) + (1,) * (len(extent) - axis_at - 1))

    factor_of = one(*split[0])
    for cut in split[1:]:
        factor_of = factor_of * one(*cut)
    return factor_of


def bell_draw(rng, shape, scale, most, cuts=(), kind=jnp.bfloat16):
    drawn = scale * jax.random.normal(rng, shape, jnp.float32)
    if cuts:
        drawn = drawn * steps_of(rng, shape, cuts, -0.22, 0.18)
    return jnp.clip(drawn, -most, most).astype(kind)


def setup_inputs(seed: int = 0) -> dict:
    streams_of = jax.random.split(jax.random.key(seed), 3)
    return {
        "kernel": draw_kernel(jax.random.fold_in(streams_of[2], 71), 0),
        "targets": bell_draw(streams_of[1], (ORDER, RHS), 1.0, 6.0, ((0, 16),), jnp.float32),
    }


def to_matrix(stored):
    order = stored.shape[0]
    return stored.reshape(N_ROW, ROW_BLOCKS, BLOCK, N_COL, COL_BLOCKS, BLOCK).transpose(1, 0, 2, 4, 3, 5).reshape(order, order)

def to_storage(matrix):
    order = matrix.shape[0]
    return matrix.reshape(ROW_BLOCKS, N_ROW, BLOCK, COL_BLOCKS, N_COL, BLOCK).transpose(1, 0, 2, 4, 3, 5).reshape(order, order)

def reference(kernel, targets):
    order = kernel.shape[0]
    width = targets.shape[1]
    natural = to_matrix(kernel)
    right = targets.reshape(N_ROW, ROW_BLOCKS, BLOCK, width).transpose(1, 0, 2, 3).reshape(order, width)
    for step in range(PANELS):
        low = step * BLOCK
        high = low + BLOCK
        factor = jnp.linalg.cholesky(natural[low:high, low:high])
        below = jax.scipy.linalg.solve_triangular(factor, natural[high:, low:high].T, lower=True).T
        natural = natural.at[high:, high:].add(-jnp.dot(below, below.T, precision=lax.Precision.HIGHEST))
        column = jnp.concatenate([jnp.zeros((low, BLOCK), natural.dtype), factor, below], 0)
        natural = natural.at[:, low:high].set(column)
        natural = natural.at[low:high, high:].set(0.0)
        answer = jax.scipy.linalg.solve_triangular(factor, right[low:high], lower=True)
        right = right.at[high:].add(-jnp.dot(below, answer, precision=lax.Precision.HIGHEST))
        right = right.at[low:high].set(answer)
    stored_rhs = right.reshape(ROW_BLOCKS, N_ROW, BLOCK, width).transpose(1, 0, 2, 3).reshape(order, width)
    return (to_storage(natural), stored_rhs)
```

```python
import jax
import jax.numpy as jnp
from jax import lax
from jax.sharding import PartitionSpec as P

BLOCK = 128
PANELS = 4
X, Y = 4, 8
ROWS, COLS = 16, 32
HI = lax.Precision.HIGHEST


def swap_by(bits, stack, axis):
    for bit in (1, 2):
        order = [i ^ bit for i in range(4)]
        parts = [lax.index_in_dim(stack, i, axis) for i in order]
        stack = jnp.where((bits & bit) != 0, jnp.concatenate(parts, axis), stack)
    return stack


def over_col(value, pairs):
    return lax.ppermute(value, "col", pairs)


def over_row(value, pairs):
    return lax.ppermute(value, "row", pairs)


def per_device(kernel, targets):
    row_pos = lax.axis_index("row")
    col_pos = lax.axis_index("col")
    x_pos = col_pos // Y
    y_pos = col_pos % Y
    block = BLOCK

    a0 = jnp.where((col_pos < 4) & (row_pos < 4), kernel[:block, :block], 0.0)
    got = [a0]
    for x in range(X):
        for half in (0, 4):
            if x or half:
                pairs = [
                    (r * COLS + j, r * COLS + x * Y + half + j)
                    for r in range(4)
                    for j in range(4)
                ]
                got.append(lax.ppermute(a0, ("row", "col"), pairs))
    a1 = sum(got[1:], got[0])
    got = [a1]
    for shift in (4, 8, 12):
        got.append(over_row(a1, [(r, r + shift) for r in range(4)]))
    a2 = sum(got[1:], got[0])
    got = [a2]
    for t in (1, 2, 3):
        got.append(over_col(a2, [(c, c ^ t) for c in range(COLS)]))
    a3 = jnp.stack(got)
    a4 = jnp.stack([a3, over_row(a3, [(r, r ^ 2) for r in range(ROWS)])])
    a5 = jnp.stack([a4, over_row(a4, [(r, r ^ 1) for r in range(ROWS)])], axis=1)
    a6 = a5.reshape(4, 4, block, block)
    a6 = swap_by(row_pos % 4, a6, 0)
    a6 = swap_by(col_pos % 4, a6, 1)
    diag = a6.transpose(0, 2, 1, 3).reshape(4 * block, 4 * block)

    panel = kernel[:, :block].reshape(8, block, block)
    got = [jnp.where(x_pos == 0, panel[:2], 0.0)]
    for x in (1, 2, 3):
        got.append(over_col(panel[2 * x : 2 * x + 2], [(j, x * Y + j) for j in range(4)]))
    shard = sum(got[1:], got[0])
    upper = over_col(shard, [(x * Y + j, x * Y + j + 4) for x in range(X) for j in range(4)])
    shard = jnp.where(y_pos >= 4, upper, shard)
    by_y = [shard]
    for t in (1, 2, 3):
        by_y.append(over_col(shard, [(c, c ^ t) for c in range(COLS)]))
    by_x = [by_y]
    for s in (1, 2, 3):
        by_x.append([over_col(part, [(c, c ^ (8 * s)) for c in range(COLS)]) for part in by_y])
    pan = jnp.stack([jnp.stack(part) for part in by_x])
    pan = swap_by(x_pos, pan, 0)
    pan = swap_by(col_pos % 4, pan, 1)
    pan = pan.transpose(0, 2, 3, 1, 4).reshape(8 * block, 4 * block)

    strip = jnp.concatenate([kernel[:block], targets[:block]], axis=1)
    got = [jnp.where(row_pos < 4, strip, 0.0)]
    for shift in (4, 8, 12):
        got.append(over_row(strip, [(r, r + shift) for r in range(4)]))
    s1 = sum(got[1:], got[0])
    s2 = jnp.stack([s1, over_row(s1, [(r, r ^ 2) for r in range(ROWS)])])
    s3 = jnp.stack([s2, over_row(s2, [(r, r ^ 1) for r in range(ROWS)])], axis=1)
    s4 = swap_by(row_pos % 4, s3.reshape(4, block, -1), 0).reshape(4 * block, -1)
    top = s4[:, :512]
    rhs = s4[:, 512:]

    factor = jnp.linalg.cholesky(diag)
    inverse = jax.scipy.linalg.solve_triangular(
        factor, jnp.eye(4 * block, dtype=jnp.float32), lower=True
    )
    w_rows = jnp.dot(pan, inverse.T, precision=HI)
    own = lax.dynamic_slice_in_dim(factor, (row_pos % 4) * block, block, 0)
    is_top = row_pos < 4
    w_rows = w_rows.at[:block].set(jnp.where(is_top, own, w_rows[:block]))
    w_cols = jnp.dot(inverse, top, precision=HI)
    z = jnp.dot(inverse, rhs, precision=HI)
    rows_in = (jnp.arange(1024) < block) & is_top
    cols_in = (jnp.arange(512) < block) & (col_pos < 4)
    trail = jnp.where(rows_in[:, None], 0.0, kernel - jnp.dot(w_rows, w_cols, precision=HI))
    mine = lax.dynamic_slice_in_dim(w_rows, (col_pos % 4) * block, block, 1)
    mine = jnp.concatenate([mine, jnp.zeros((1024, 384), jnp.float32)], axis=1)
    out = jnp.where(cols_in[None, :], mine, trail)
    z_own = lax.dynamic_slice_in_dim(z, (row_pos % 4) * block, block, 0)
    z_own = jnp.concatenate([z_own, jnp.zeros((896, 128), jnp.float32)], axis=0)
    right = jnp.where(rows_in[:, None], z_own, targets - jnp.dot(w_rows, z, precision=HI))
    return out, right


def solution(mesh):
    in_specs = (P("row", "col"), P("row", None))
    out_specs = (P("row", "col"), P("row", None))
    return jax.shard_map(
        per_device, mesh=mesh, in_specs=in_specs, out_specs=out_specs, check_vma=False
    )
```

```python
import jax
import jax.numpy as jnp
from jax import lax
from jax.experimental import pallas as pl
from jax.experimental.pallas import tpu as pltpu
from jax.sharding import PartitionSpec as P

BLOCK = 128
ORDER = 512
X, Y = 4, 8
ROWS, COLS = 16, 32
HI = lax.Precision.HIGHEST


def over_col(value, pairs):
    return lax.ppermute(value, "col", pairs)


def over_row(value, pairs):
    return lax.ppermute(value, "row", pairs)


def dot(a, b):
    return lax.dot_general(
        a, b, (((1,), (0,)), ((), ())), precision=HI, preferred_element_type=jnp.float32
    )


def dot_nt(a, b):
    return lax.dot_general(
        a, b, (((1,), (1,)), ((), ())), precision=HI, preferred_element_type=jnp.float32
    )


def spread(value):
    return jnp.broadcast_to(value, (8, BLOCK))


def total(terms):
    terms = list(terms)
    while len(terms) > 1:
        terms = [sum(terms[i + 1 : i + 2], terms[i]) for i in range(0, len(terms), 2)]
    return terms[0]


def factor_block(s_ref, e_ref):
    ids = lax.broadcasted_iota(jnp.int32, (BLOCK, BLOCK), 0)
    lanes = lax.broadcasted_iota(jnp.int32, (BLOCK, BLOCK), 1)
    e_ref[...] = jnp.where(ids == lanes, 1.0, 0.0)
    sub = lax.broadcasted_iota(jnp.int32, (8, BLOCK), 0)
    for p in range(16):
        at = 8 * p
        own = s_ref[at : at + 8, :]
        own_e = e_ref[at : at + 8, :]
        cols = [spread(own[:, at + i : at + i + 1]) for i in range(8)]
        t = {(s, i): spread(cols[i][s : s + 1, :]) for i in range(8) for s in range(i, 8)}
        rows = [spread(own[q : q + 1, :]) for q in range(8)]
        rows_e = [spread(own_e[q : q + 1, :]) for q in range(8)]
        low, inv, root = {}, {}, []
        for i in range(8):
            rs = lax.rsqrt(t[i, i])
            root.append(rs)
            for s in range(i + 1, 8):
                low[s, i] = t[s, i] * rs
            for s in range(i + 1, 8):
                for q in range(i + 1, s + 1):
                    t[s, q] = t[s, q] - low[s, i] * low[q, i]
        for i in range(8):
            inv[i, i] = root[i]
            for s in range(i + 1, 8):
                inv[s, i] = -root[s] * total(low[s, q] * inv[q, i] for q in range(i, s))
        done = [total(inv[i, q] * rows[q] for q in range(i + 1)) for i in range(8)]
        done_e = [total(inv[i, q] * rows_e[q] for q in range(i + 1)) for i in range(8)]
        tile, tile_e = done[0], done_e[0]
        for i in range(1, 8):
            tile = jnp.where(sub == i, done[i], tile)
            tile_e = jnp.where(sub == i, done_e[i], tile_e)
        s_ref[at : at + 8, :] = tile
        e_ref[at : at + 8, :] = tile_e
        if p == 15:
            break
        back = [total(inv[i, j] * done[i] for i in range(j, 8)) for j in range(8)]
        back_e = [total(inv[i, j] * done_e[i] for i in range(j, 8)) for j in range(8)]
        for u in range(p + 1, 16):
            part = s_ref[8 * u : 8 * u + 8, :]
            left = [spread(part[:, at + j : at + j + 1]) for j in range(8)]
            s_ref[8 * u : 8 * u + 8, :] = part - total(left[j] * back[j] for j in range(8))
            e_ref[8 * u : 8 * u + 8, :] -= total(left[j] * back_e[j] for j in range(8))


def factor_kernel(at_ref, a_ref, f_ref, g_ref, work, s_ref, e_ref):
    k = pl.program_id(0)
    n = BLOCK

    @pl.when(k == 0)
    def _():
        for i in range(4):
            for j in range(i + 1):
                work[i * n : (i + 1) * n, j * n : (j + 1) * n] = a_ref[
                    at_ref[0] ^ i, at_ref[1] ^ j
                ]
        f_ref[...] = jnp.zeros_like(f_ref)
        g_ref[...] = jnp.zeros_like(g_ref)

    for step in range(4):
        @pl.when(k == step)
        def _(step=step):
            here = slice(step * n, (step + 1) * n)
            s_ref[...] = work[here, here]

    factor_block(s_ref, e_ref)

    for step in range(4):
        @pl.when(k == step)
        def _(step=step):
            here = slice(step * n, (step + 1) * n)
            ids = lax.broadcasted_iota(jnp.int32, (n, n), 0)
            lanes = lax.broadcasted_iota(jnp.int32, (n, n), 1)
            f_ref[here, here] = jnp.where(ids <= lanes, s_ref[...], 0.0).T
            inv = e_ref[...]
            g_ref[here, here] = inv
            if step < 3:
                f_ref[(step + 1) * n :, here] = dot_nt(work[(step + 1) * n :, here], inv)
            for j in range(step + 1, 4):
                there = slice(j * n, (j + 1) * n)
                work[j * n :, there] -= dot_nt(f_ref[j * n :, here], f_ref[there, here])
            if step:
                before = slice(0, step * n)
                g_ref[here, before] = -dot(inv, dot(f_ref[here, before], g_ref[before, before]))


def factor(at, blocks):
    return pl.pallas_call(
        factor_kernel,
        grid=(4,),
        out_shape=[jax.ShapeDtypeStruct((ORDER, ORDER), jnp.float32)] * 2,
        in_specs=[
            pl.BlockSpec(memory_space=pltpu.SMEM),
            pl.BlockSpec((4, 4, BLOCK, BLOCK), lambda k: (0, 0, 0, 0)),
        ],
        out_specs=[pl.BlockSpec((ORDER, ORDER), lambda k: (0, 0))] * 2,
        scratch_shapes=[
            pltpu.VMEM((ORDER, ORDER), jnp.float32),
            pltpu.VMEM((BLOCK, BLOCK), jnp.float32),
            pltpu.VMEM((BLOCK, BLOCK), jnp.float32),
        ],
        compiler_params=pltpu.CompilerParams(vmem_limit_bytes=24 * 2**20),
        cost_estimate=pl.CostEstimate(flops=2 * 10**10, bytes_accessed=3 * 2**20, transcendentals=0),
    )(at, blocks)


def update_kernel(at_ref, pan_ref, top_ref, f_ref, g_ref, k_ref, y_ref, out_ref, right_ref,
                  wc, tmp, pan, w):
    step = pl.program_id(0)
    row, col = at_ref[2], at_ref[3]
    n = BLOCK

    @pl.when(step == 0)
    def _():
        for i in range(4):
            tmp[i * n : (i + 1) * n, :] = top_ref[at_ref[0] ^ i]
        for i in range(4):
            here = slice(i * n, (i + 1) * n)
            wc[here, :] = dot(g_ref[here, : (i + 1) * n], tmp[: (i + 1) * n, :])

    for j in range(4):
        for b in range(2):
            pan[b * n : (b + 1) * n, j * n : (j + 1) * n] = pan_ref[0, b, j]
    for i in range(4):
        here = slice(i * n, (i + 1) * n)
        w[:, here] = dot_nt(pan[:, : (i + 1) * n], g_ref[here, : (i + 1) * n])

    first = (step == 0) & (row < 4)

    @pl.when(first)
    def _():
        w[:n, :] = f_ref[pl.ds(pl.multiple_of(row * n, n), n), :]

    out_ref[...] = k_ref[...] - dot(w[...], wc[:, :ORDER])
    right_ref[...] = y_ref[...] - dot(w[...], wc[:, ORDER:])

    @pl.when(first)
    def _():
        out_ref[:n, :] = jnp.zeros((n, ORDER), jnp.float32)
        right_ref[:n, :] = wc[pl.ds(pl.multiple_of(row * n, n), n), ORDER:]

    @pl.when(col < 4)
    def _():
        out_ref[:, :n] = w[:, pl.ds(pl.multiple_of(col * n, n), n)]


def update(at, pan, top, fac, inv, kernel, targets):
    rows = 256
    whole = lambda *shape: pl.BlockSpec(shape, lambda s: (0,) * len(shape))
    return pl.pallas_call(
        update_kernel,
        grid=(kernel.shape[0] // rows,),
        out_shape=[
            jax.ShapeDtypeStruct(kernel.shape, jnp.float32),
            jax.ShapeDtypeStruct(targets.shape, jnp.float32),
        ],
        in_specs=[
            pl.BlockSpec(memory_space=pltpu.SMEM),
            pl.BlockSpec((1, 2, 4, BLOCK, BLOCK), lambda s: (s, 0, 0, 0, 0)),
            whole(4, BLOCK, ORDER + BLOCK),
            whole(ORDER, ORDER),
            whole(ORDER, ORDER),
            pl.BlockSpec((rows, ORDER), lambda s: (s, 0)),
            pl.BlockSpec((rows, BLOCK), lambda s: (s, 0)),
        ],
        out_specs=[
            pl.BlockSpec((rows, ORDER), lambda s: (s, 0)),
            pl.BlockSpec((rows, BLOCK), lambda s: (s, 0)),
        ],
        scratch_shapes=[
            pltpu.VMEM((ORDER, ORDER + BLOCK), jnp.float32),
            pltpu.VMEM((ORDER, ORDER + BLOCK), jnp.float32),
            pltpu.VMEM((rows, ORDER), jnp.float32),
            pltpu.VMEM((rows, ORDER), jnp.float32),
        ],
        compiler_params=pltpu.CompilerParams(vmem_limit_bytes=40 * 2**20),
        cost_estimate=pl.CostEstimate(flops=10**10, bytes_accessed=9 * 2**20, transcendentals=0),
    )(at, pan, top, fac, inv, kernel, targets)


def per_device(kernel, targets):
    row_pos = lax.axis_index("row")
    col_pos = lax.axis_index("col")
    x_pos = col_pos // Y
    y_pos = col_pos % Y
    block = BLOCK
    at = jnp.stack([row_pos % 4, col_pos % 4, row_pos, col_pos]).astype(jnp.int32)

    a0 = jnp.where((col_pos < 4) & (row_pos < 4), kernel[:block, :block], 0.0)
    got = [a0]
    for x in range(X):
        for half in (0, 4):
            if x or half:
                pairs = [
                    (r * COLS + j, r * COLS + x * Y + half + j)
                    for r in range(4)
                    for j in range(4)
                ]
                got.append(lax.ppermute(a0, ("row", "col"), pairs))
    a1 = total(got)
    got = [a1]
    for shift in (4, 8, 12):
        got.append(over_row(a1, [(r, r + shift) for r in range(4)]))
    a2 = total(got)
    got = [a2]
    for t in (1, 2, 3):
        got.append(over_col(a2, [(c, c ^ t) for c in range(COLS)]))
    a3 = jnp.stack(got)
    a4 = jnp.stack([a3, over_row(a3, [(r, r ^ 2) for r in range(ROWS)])])
    a5 = jnp.stack([a4, over_row(a4, [(r, r ^ 1) for r in range(ROWS)])], axis=1)
    fac, inv = factor(at, a5.reshape(4, 4, block, block))

    panel = kernel[:, :block].reshape(8, block, block)
    got = [jnp.where(x_pos == 0, panel[:2], 0.0)]
    for x in (1, 2, 3):
        got.append(over_col(panel[2 * x : 2 * x + 2], [(j, x * Y + j) for j in range(4)]))
    pair = total(got)
    upper = over_col(pair[1], [(x * Y + j, x * Y + j + 4) for x in range(X) for j in range(4)])
    shard = jnp.where(y_pos >= 4, upper, pair[0])
    pan = lax.all_gather(shard, "col").reshape(4, 2, 4, block, block)

    strip = jnp.concatenate([kernel[:block], targets[:block]], axis=1)
    got = [jnp.where(row_pos < 4, strip, 0.0)]
    for shift in (4, 8, 12):
        got.append(over_row(strip, [(r, r + shift) for r in range(4)]))
    s1 = total(got)
    s2 = jnp.stack([s1, over_row(s1, [(r, r ^ 2) for r in range(ROWS)])])
    s3 = jnp.stack([s2, over_row(s2, [(r, r ^ 1) for r in range(ROWS)])], axis=1)
    top = s3.reshape(4, block, ORDER + block)

    return tuple(update(at, pan, top, fac, inv, kernel, targets))


def solution(mesh):
    in_specs = (P("row", "col"), P("row", None))
    out_specs = (P("row", "col"), P("row", None))
    return jax.shard_map(
        per_device, mesh=mesh, in_specs=in_specs, out_specs=out_specs, check_vma=False
    )
```

```python
import functools

import jax
import jax.numpy as jnp
from jax import lax
from jax.experimental import pallas as pl
from jax.experimental.pallas import tpu as pltpu
from jax.sharding import PartitionSpec as P

BLOCK = 128
ORDER = 512
X, Y = 4, 8
ROWS, COLS = 16, 32
HI = lax.Precision.HIGHEST


def over_col(value, pairs):
    return lax.ppermute(value, "col", pairs)


def over_row(value, pairs):
    return lax.ppermute(value, "row", pairs)


def dot(a, b):
    return lax.dot_general(
        a, b, (((1,), (0,)), ((), ())), precision=HI, preferred_element_type=jnp.float32
    )


def dot_nt(a, b):
    return lax.dot_general(
        a, b, (((1,), (1,)), ((), ())), precision=HI, preferred_element_type=jnp.float32
    )


def spread(value):
    return jnp.broadcast_to(value, (8, BLOCK))


def total(terms):
    terms = list(terms)
    while len(terms) > 1:
        terms = [sum(terms[i + 1 : i + 2], terms[i]) for i in range(0, len(terms), 2)]
    return terms[0]


def factor_block(s_ref, e_ref):
    ids = lax.broadcasted_iota(jnp.int32, (BLOCK, BLOCK), 0)
    lanes = lax.broadcasted_iota(jnp.int32, (BLOCK, BLOCK), 1)
    e_ref[...] = jnp.where(ids == lanes, 1.0, 0.0)
    sub = lax.broadcasted_iota(jnp.int32, (8, BLOCK), 0)
    for p in range(16):
        at = 8 * p
        own = s_ref[at : at + 8, :]
        own_e = e_ref[at : at + 8, :]
        cols = [spread(own[:, at + i : at + i + 1]) for i in range(8)]
        t = {(s, i): spread(cols[i][s : s + 1, :]) for i in range(8) for s in range(i, 8)}
        rows = [spread(own[q : q + 1, :]) for q in range(8)]
        rows_e = [spread(own_e[q : q + 1, :]) for q in range(8)]
        low, inv, root = {}, {}, []
        for i in range(8):
            rs = lax.rsqrt(t[i, i])
            root.append(rs)
            for s in range(i + 1, 8):
                low[s, i] = t[s, i] * rs
            for s in range(i + 1, 8):
                for q in range(i + 1, s + 1):
                    t[s, q] = t[s, q] - low[s, i] * low[q, i]
        for i in range(8):
            inv[i, i] = root[i]
            for s in range(i + 1, 8):
                inv[s, i] = -root[s] * total(low[s, q] * inv[q, i] for q in range(i, s))
        done = [total(inv[i, q] * rows[q] for q in range(i + 1)) for i in range(8)]
        done_e = [total(inv[i, q] * rows_e[q] for q in range(i + 1)) for i in range(8)]
        tile, tile_e = done[0], done_e[0]
        for i in range(1, 8):
            tile = jnp.where(sub == i, done[i], tile)
            tile_e = jnp.where(sub == i, done_e[i], tile_e)
        s_ref[at : at + 8, :] = tile
        e_ref[at : at + 8, :] = tile_e
        if p == 15:
            break
        back = [total(inv[i, j] * done[i] for i in range(j, 8)) for j in range(8)]
        back_e = [total(inv[i, j] * done_e[i] for i in range(j, 8)) for j in range(8)]
        for u in range(p + 1, 16):
            part = s_ref[8 * u : 8 * u + 8, :]
            left = [spread(part[:, at + j : at + j + 1]) for j in range(8)]
            s_ref[8 * u : 8 * u + 8, :] = part - total(left[j] * back[j] for j in range(8))
            e_ref[8 * u : 8 * u + 8, :] -= total(left[j] * back_e[j] for j in range(8))


def invert_block(work, s_ref, e_ref, k):
    n = BLOCK
    here = slice(k * n, (k + 1) * n)
    s_ref[...] = work[here, here]
    factor_block(s_ref, e_ref)
    ids = lax.broadcasted_iota(jnp.int32, (n, n), 0)
    lanes = lax.broadcasted_iota(jnp.int32, (n, n), 1)
    return jnp.where(ids <= lanes, s_ref[...], 0.0).T, e_ref[...]


def first_kernel(at_ref, own_ref, got_ref, f_ref, g_ref, rest_ref, work, s_ref, e_ref):
    n = BLOCK
    for i in range(4):
        u = at_ref[0] ^ i
        for j in range(i + 1):
            t = at_ref[1] ^ j
            work[i * n : (i + 1) * n, j * n : (j + 1) * n] = jnp.where(
                u % 2 == 0,
                own_ref[u // 2, t % 2, t // 2],
                got_ref[u // 2, t % 2, t // 2],
            )
    fac, inv = invert_block(work, s_ref, e_ref, 0)
    f_ref[:n, :] = fac
    g_ref[...] = inv
    f_ref[n:, :] = dot_nt(work[n:, :n], inv)
    for j in range(1, 4):
        rest_ref[(j - 1) * n :, (j - 1) * n : j * n] = work[
            j * n :, j * n : (j + 1) * n
        ] - dot_nt(f_ref[j * n :, :], f_ref[j * n : (j + 1) * n, :])


def second_kernel(f0_ref, g0_ref, rest_ref, f_ref, g_ref, work, s_ref, e_ref):
    k = pl.program_id(0) + 1
    n = BLOCK

    @pl.when(k == 1)
    def _():
        f_ref[...] = jnp.zeros_like(f_ref)
        g_ref[...] = jnp.zeros_like(g_ref)
        f_ref[:, :n] = f0_ref[...]
        g_ref[:n, :n] = g0_ref[...]
        for j in range(1, 4):
            there = slice(j * n, (j + 1) * n)
            work[j * n :, there] = rest_ref[(j - 1) * n :, (j - 1) * n : j * n]

    for step in range(1, 4):
        @pl.when(k == step)
        def _(step=step):
            here = slice(step * n, (step + 1) * n)
            s_ref[...] = work[here, here]

    factor_block(s_ref, e_ref)

    for step in range(1, 4):
        @pl.when(k == step)
        def _(step=step):
            here = slice(step * n, (step + 1) * n)
            ids = lax.broadcasted_iota(jnp.int32, (n, n), 0)
            lanes = lax.broadcasted_iota(jnp.int32, (n, n), 1)
            f_ref[here, here] = jnp.where(ids <= lanes, s_ref[...], 0.0).T
            inv = e_ref[...]
            g_ref[here, here] = inv
            if step < 3:
                f_ref[(step + 1) * n :, here] = dot_nt(work[(step + 1) * n :, here], inv)
            for j in range(step + 1, 4):
                there = slice(j * n, (j + 1) * n)
                work[j * n :, there] -= dot_nt(f_ref[j * n :, here], f_ref[there, here])
            before = slice(0, step * n)
            g_ref[here, before] = -dot(inv, dot(f_ref[here, before], g_ref[before, before]))


def f32(*shape):
    return jax.ShapeDtypeStruct(shape, jnp.float32)


VMEM = pl.BlockSpec(memory_space=pltpu.VMEM)
SMEM = pl.BlockSpec(memory_space=pltpu.SMEM)
WORK = [
    pltpu.VMEM((ORDER, ORDER), jnp.float32),
    pltpu.VMEM((BLOCK, BLOCK), jnp.float32),
    pltpu.VMEM((BLOCK, BLOCK), jnp.float32),
]


def factor_first(at, own, got):
    return pl.pallas_call(
        first_kernel,
        out_shape=[f32(ORDER, BLOCK), f32(BLOCK, BLOCK), f32(ORDER - BLOCK, ORDER - BLOCK)],
        in_specs=[SMEM, VMEM, VMEM],
        out_specs=[VMEM] * 3,
        scratch_shapes=WORK,
        compiler_params=pltpu.CompilerParams(vmem_limit_bytes=8 * 2**20),
        cost_estimate=pl.CostEstimate(flops=6 * 10**9, bytes_accessed=2**20, transcendentals=0),
    )(at, own, got)


def factor_rest(f0, g0, rest):
    return pl.pallas_call(
        second_kernel,
        grid=(3,),
        out_shape=[f32(ORDER, ORDER)] * 2,
        in_specs=[VMEM] * 3,
        out_specs=[VMEM] * 2,
        scratch_shapes=WORK,
        compiler_params=pltpu.CompilerParams(vmem_limit_bytes=8 * 2**20),
        cost_estimate=pl.CostEstimate(flops=18 * 10**9, bytes_accessed=2**20, transcendentals=0),
    )(f0, g0, rest)


def strip_kernel(top_ref, g_ref, wc_ref, tmp):
    n = BLOCK
    for i in range(4):
        for a in range(4):
            tmp[i * n + a * 32 : i * n + (a + 1) * 32, :] = top_ref[4 * a + i]
    for i in range(4):
        here = slice(i * n, (i + 1) * n)
        wc_ref[here, :] = dot(g_ref[here, : (i + 1) * n], tmp[: (i + 1) * n, :])


def strip_solve(top, inv):
    shape = (ORDER, ORDER + BLOCK)
    return pl.pallas_call(
        strip_kernel,
        out_shape=f32(*shape),
        in_specs=[VMEM] * 2,
        out_specs=VMEM,
        scratch_shapes=[pltpu.VMEM(shape, jnp.float32)],
        compiler_params=pltpu.CompilerParams(vmem_limit_bytes=8 * 2**20),
        cost_estimate=pl.CostEstimate(flops=4 * 10**9, bytes_accessed=4 * 2**20, transcendentals=0),
    )(top, inv)


def update_kernel(at_ref, q0_ref, q1_ref, q2_ref, low_ref, high_ref, f_ref, g_ref, wc_ref,
                  k_ref, y_ref, out_ref, right_ref, pan, w):
    step = pl.program_id(0)
    row, col = at_ref[2], at_ref[3]
    n = BLOCK

    def fill(read):
        for j in range(4):
            t = at_ref[1] ^ j
            for b in range(2):
                pan[b * n : (b + 1) * n, j * n : (j + 1) * n] = read(t % 2, t // 2, b)

    for s, ref in enumerate((q0_ref, q1_ref, q2_ref)):
        @pl.when(step == s)
        def _(ref=ref):
            fill(lambda t1, t2, b: ref[t1, t2, b])

    @pl.when(step == 3)
    def _():
        fill(lambda t1, t2, b: jnp.where(t1 == 0, low_ref[t2, b], high_ref[t2, b]))

    for i in range(4):
        here = slice(i * n, (i + 1) * n)
        w[:, here] = dot_nt(pan[:, : (i + 1) * n], g_ref[here, : (i + 1) * n])

    first = (at_ref[4 + step] == 0) & (row < 4)

    @pl.when(first)
    def _():
        w[:n, :] = f_ref[pl.ds(pl.multiple_of(row * n, n), n), :]

    out_ref[...] = k_ref[...] - dot(w[...], wc_ref[:, :ORDER])
    right_ref[...] = y_ref[...] - dot(w[...], wc_ref[:, ORDER:])

    @pl.when(first)
    def _():
        out_ref[:n, :] = jnp.zeros((n, ORDER), jnp.float32)
        right_ref[:n, :] = wc_ref[pl.ds(pl.multiple_of(row * n, n), n), ORDER:]

    @pl.when(col < 4)
    def _():
        out_ref[:, :n] = w[:, pl.ds(pl.multiple_of(col * n, n), n)]


def update(at, parts, fac, inv, wc, kernel, targets):
    rows = 256
    moved = lambda width: pl.BlockSpec((rows, width), lambda s, at: (at[4 + s], 0))
    return pl.pallas_call(
        update_kernel,
        out_shape=[f32(*kernel.shape), f32(*targets.shape)],
        grid_spec=pltpu.PrefetchScalarGridSpec(
            num_scalar_prefetch=1,
            grid=(4,),
            in_specs=[VMEM] * 8 + [moved(ORDER), moved(BLOCK)],
            out_specs=[moved(ORDER), moved(BLOCK)],
            scratch_shapes=[pltpu.VMEM((rows, ORDER), jnp.float32)] * 2,
        ),
        compiler_params=pltpu.CompilerParams(vmem_limit_bytes=16 * 2**20),
        cost_estimate=pl.CostEstimate(flops=10**10, bytes_accessed=6 * 2**20, transcendentals=0),
    )(at, *parts, fac, inv, wc, kernel, targets)


def after(value, *others):
    return lax.optimization_barrier((value, *others))[0]


def per_device(kernel, targets):
    row_pos = lax.axis_index("row")
    col_pos = lax.axis_index("col")
    x_pos = col_pos // Y
    y_pos = col_pos % Y
    n = BLOCK
    base = jnp.where(y_pos < 4, y_pos, 7 - y_pos)
    shifts = jnp.array([0, 3, 1, 2], jnp.int32)
    at = jnp.concatenate(
        [jnp.stack([row_pos % 4, base, row_pos, col_pos]), (x_pos + shifts) % 4]
    ).astype(jnp.int32)
    mirror = [(x * Y + j, x * Y + 7 - j) for x in range(X) for j in range(4)]
    by_two = [(c, c ^ 2) for c in range(COLS)]
    by_one = [(c, c ^ 1) for c in range(COLS)]

    a0 = jnp.where((col_pos < 4) & (row_pos < 4), kernel[:n, :n], 0.0)
    got = [a0]
    for x in (1, 2, 3):
        pairs = [(r * COLS + j, r * COLS + x * Y + j) for r in range(4) for j in range(4)]
        got.append(lax.ppermute(a0, ("row", "col"), pairs))
    a1 = total(got)

    strip = jnp.concatenate([kernel[:n], targets[:n]], axis=1)
    got = [jnp.where(row_pos < 4, strip[:32], 0.0)]
    for a in (1, 2, 3):
        got.append(over_row(strip[32 * a : 32 * a + 32], [(r, r + 4 * a) for r in range(4)]))
    piece = total(got)
    top = lax.all_gather(piece, "row")

    panel = kernel[:, :n].reshape(8, n, n)
    got = [jnp.where(x_pos == 0, panel[:2], 0.0)]
    for x in (1, 2, 3):
        got.append(over_col(panel[2 * x : 2 * x + 2], [(j, x * Y + j) for j in range(4)]))
    p1 = total(got)

    a2 = after(a1 + over_col(a1, mirror), piece, p1)
    got = [a2]
    for a in (1, 2, 3):
        got.append(over_row(a2, [(r, r + 4 * a) for r in range(4)]))
    a3 = total(got)
    p2 = jnp.where(y_pos >= 4, over_col(after(p1, a2), mirror), p1)
    a4 = jnp.stack([a3, over_col(a3, by_two)])
    a5 = jnp.stack([a4, over_col(a4, by_one)])
    p3 = jnp.stack([p2, over_col(after(p2, a5), by_two)])
    a6 = jnp.stack([a5, over_row(a5, [(r, r ^ 2) for r in range(ROWS)])])
    p4 = jnp.stack([p3, over_col(after(p3, a6), by_one)])
    a7 = over_row(a6, [(r, r ^ 1) for r in range(ROWS)])

    state = factor_first(at, a6, a7)
    p4 = after(p4, state[1])
    down = over_col(p4, [(c, (c + Y) % COLS) for c in range(COLS)])
    up = over_col(p4, [(c, (c - Y) % COLS) for c in range(COLS)])
    fac, inv = factor_rest(*state)
    low = over_col(after(up[0], inv), [(c, (c - Y) % COLS) for c in range(COLS)])
    high = over_col(after(down[1], inv), [(c, (c + Y) % COLS) for c in range(COLS)])
    wc = strip_solve(top, inv)
    return tuple(update(at, (p4, down, up, low, high), fac, inv, wc, kernel, targets))


def solution(mesh):
    in_specs = (P("row", "col"), P("row", None))
    out_specs = (P("row", "col"), P("row", None))
    return jax.shard_map(
        per_device, mesh=mesh, in_specs=in_specs, out_specs=out_specs, check_vma=False
    )
```

```python
import functools

import jax
import jax.numpy as jnp
from jax import lax
from jax.experimental import pallas as pl
from jax.experimental.pallas import tpu as pltpu
from jax.sharding import PartitionSpec as P

BLOCK = 128
ORDER = 512
X, Y = 4, 8
ROWS, COLS = 16, 32
HI = lax.Precision.HIGHEST


def over_col(value, pairs):
    return lax.ppermute(value, "col", pairs)


def over_row(value, pairs):
    return lax.ppermute(value, "row", pairs)


def dot(a, b):
    return lax.dot_general(
        a, b, (((1,), (0,)), ((), ())), precision=HI, preferred_element_type=jnp.float32
    )


def dot_nt(a, b):
    return lax.dot_general(
        a, b, (((1,), (1,)), ((), ())), precision=HI, preferred_element_type=jnp.float32
    )


def spread(value):
    return jnp.broadcast_to(value, (8, BLOCK))


def total(terms):
    terms = list(terms)
    while len(terms) > 1:
        terms = [sum(terms[i + 1 : i + 2], terms[i]) for i in range(0, len(terms), 2)]
    return terms[0]


def factor_block(s_ref, e_ref):
    ids = lax.broadcasted_iota(jnp.int32, (BLOCK, BLOCK), 0)
    lanes = lax.broadcasted_iota(jnp.int32, (BLOCK, BLOCK), 1)
    e_ref[...] = jnp.where(ids == lanes, 1.0, 0.0)
    sub = lax.broadcasted_iota(jnp.int32, (8, BLOCK), 0)
    for p in range(16):
        at = 8 * p
        own = s_ref[at : at + 8, :]
        own_e = e_ref[at : at + 8, :]
        cols = [spread(own[:, at + i : at + i + 1]) for i in range(8)]
        t = {(s, i): spread(cols[i][s : s + 1, :]) for i in range(8) for s in range(i, 8)}
        rows = [spread(own[q : q + 1, :]) for q in range(8)]
        rows_e = [spread(own_e[q : q + 1, :]) for q in range(8)]
        low, inv, root = {}, {}, []
        for i in range(8):
            rs = lax.rsqrt(t[i, i])
            root.append(rs)
            for s in range(i + 1, 8):
                low[s, i] = t[s, i] * rs
            for s in range(i + 1, 8):
                for q in range(i + 1, s + 1):
                    t[s, q] = t[s, q] - low[s, i] * low[q, i]
        for i in range(8):
            inv[i, i] = root[i]
            for s in range(i + 1, 8):
                inv[s, i] = -root[s] * total(low[s, q] * inv[q, i] for q in range(i, s))
        done = [total(inv[i, q] * rows[q] for q in range(i + 1)) for i in range(8)]
        done_e = [total(inv[i, q] * rows_e[q] for q in range(i + 1)) for i in range(8)]
        tile, tile_e = done[0], done_e[0]
        for i in range(1, 8):
            tile = jnp.where(sub == i, done[i], tile)
            tile_e = jnp.where(sub == i, done_e[i], tile_e)
        s_ref[at : at + 8, :] = tile
        e_ref[at : at + 8, :] = tile_e
        if p == 15:
            break
        back = [total(inv[i, j] * done[i] for i in range(j, 8)) for j in range(8)]
        back_e = [total(inv[i, j] * done_e[i] for i in range(j, 8)) for j in range(8)]
        for u in range(p + 1, 16):
            part = s_ref[8 * u : 8 * u + 8, :]
            left = [spread(part[:, at + j : at + j + 1]) for j in range(8)]
            s_ref[8 * u : 8 * u + 8, :] = part - total(left[j] * back[j] for j in range(8))
            e_ref[8 * u : 8 * u + 8, :] -= total(left[j] * back_e[j] for j in range(8))


def invert_block(work, s_ref, e_ref, k):
    n = BLOCK
    here = slice(k * n, (k + 1) * n)
    s_ref[...] = work[here, here]
    factor_block(s_ref, e_ref)
    ids = lax.broadcasted_iota(jnp.int32, (n, n), 0)
    lanes = lax.broadcasted_iota(jnp.int32, (n, n), 1)
    return jnp.where(ids <= lanes, s_ref[...], 0.0).T, e_ref[...]


def first_kernel(at_ref, own_ref, got_ref, f_ref, g_ref, rest_ref, work, s_ref, e_ref):
    n = BLOCK
    for i in range(4):
        u = at_ref[0] ^ i
        for j in range(i + 1):
            t = at_ref[1] ^ j
            work[i * n : (i + 1) * n, j * n : (j + 1) * n] = jnp.where(
                u % 2 == 0,
                own_ref[u // 2, t % 2, t // 2],
                got_ref[u // 2, t % 2, t // 2],
            )
    fac, inv = invert_block(work, s_ref, e_ref, 0)
    f_ref[:n, :] = fac
    g_ref[...] = inv
    f_ref[n:, :] = dot_nt(work[n:, :n], inv)
    for j in range(1, 4):
        rest_ref[(j - 1) * n :, (j - 1) * n : j * n] = work[
            j * n :, j * n : (j + 1) * n
        ] - dot_nt(f_ref[j * n :, :], f_ref[j * n : (j + 1) * n, :])


def middle_kernel(f0_ref, g0_ref, rest_ref, f_ref, g_ref, left_ref, work, s_ref, e_ref):
    k = pl.program_id(0) + 1
    n = BLOCK

    @pl.when(k == 1)
    def _():
        f_ref[...] = jnp.zeros_like(f_ref)
        g_ref[...] = jnp.zeros_like(g_ref)
        f_ref[:, :n] = f0_ref[...]
        g_ref[:n, :n] = g0_ref[...]
        for j in range(1, 4):
            there = slice(j * n, (j + 1) * n)
            work[j * n :, there] = rest_ref[(j - 1) * n :, (j - 1) * n : j * n]

    for step in (1, 2):
        @pl.when(k == step)
        def _(step=step):
            here = slice(step * n, (step + 1) * n)
            s_ref[...] = work[here, here]

    factor_block(s_ref, e_ref)

    for step in (1, 2):
        @pl.when(k == step)
        def _(step=step):
            here = slice(step * n, (step + 1) * n)
            ids = lax.broadcasted_iota(jnp.int32, (n, n), 0)
            lanes = lax.broadcasted_iota(jnp.int32, (n, n), 1)
            f_ref[here, here] = jnp.where(ids <= lanes, s_ref[...], 0.0).T
            inv = e_ref[...]
            g_ref[here, here] = inv
            f_ref[(step + 1) * n :, here] = dot_nt(work[(step + 1) * n :, here], inv)
            for j in range(step + 1, 4):
                there = slice(j * n, (j + 1) * n)
                work[j * n :, there] -= dot_nt(f_ref[j * n :, here], f_ref[there, here])
            before = slice(0, step * n)
            g_ref[here, before] = -dot(inv, dot(f_ref[here, before], g_ref[before, before]))
            if step == 2:
                left_ref[...] = work[3 * n :, 3 * n :]


def last_kernel(f_ref, g_ref, left_ref, f3_ref, g3_ref, s_ref, e_ref):
    n = BLOCK
    old = 3 * n
    s_ref[...] = left_ref[...]
    factor_block(s_ref, e_ref)
    ids = lax.broadcasted_iota(jnp.int32, (n, n), 0)
    lanes = lax.broadcasted_iota(jnp.int32, (n, n), 1)
    inv = e_ref[...]
    f3_ref[:, :old] = f_ref[old:, :old]
    f3_ref[:, old:] = jnp.where(ids <= lanes, s_ref[...], 0.0).T
    g3_ref[:, :old] = -dot(inv, dot(f_ref[old:, :old], g_ref[:old, :old]))
    g3_ref[:, old:] = inv


def f32(*shape):
    return jax.ShapeDtypeStruct(shape, jnp.float32)


VMEM = pl.BlockSpec(memory_space=pltpu.VMEM)
SMEM = pl.BlockSpec(memory_space=pltpu.SMEM)
WORK = [
    pltpu.VMEM((ORDER, ORDER), jnp.float32),
    pltpu.VMEM((BLOCK, BLOCK), jnp.float32),
    pltpu.VMEM((BLOCK, BLOCK), jnp.float32),
]


def factor_first(at, own, got):
    return pl.pallas_call(
        first_kernel,
        out_shape=[f32(ORDER, BLOCK), f32(BLOCK, BLOCK), f32(ORDER - BLOCK, ORDER - BLOCK)],
        in_specs=[SMEM, VMEM, VMEM],
        out_specs=[VMEM] * 3,
        scratch_shapes=WORK,
        compiler_params=pltpu.CompilerParams(vmem_limit_bytes=8 * 2**20),
        cost_estimate=pl.CostEstimate(flops=6 * 10**9, bytes_accessed=2**20, transcendentals=0),
    )(at, own, got)


def factor_middle(f0, g0, rest):
    return pl.pallas_call(
        middle_kernel,
        grid=(2,),
        out_shape=[f32(ORDER, ORDER), f32(ORDER, ORDER), f32(BLOCK, BLOCK)],
        in_specs=[VMEM] * 3,
        out_specs=[VMEM] * 3,
        scratch_shapes=WORK,
        compiler_params=pltpu.CompilerParams(vmem_limit_bytes=8 * 2**20),
        cost_estimate=pl.CostEstimate(flops=12 * 10**9, bytes_accessed=2**20, transcendentals=0),
    )(f0, g0, rest)


def factor_last(fac, inv, left):
    return pl.pallas_call(
        last_kernel,
        out_shape=[f32(BLOCK, ORDER)] * 2,
        in_specs=[VMEM] * 3,
        out_specs=[VMEM] * 2,
        scratch_shapes=WORK[1:],
        compiler_params=pltpu.CompilerParams(vmem_limit_bytes=8 * 2**20),
        cost_estimate=pl.CostEstimate(flops=6 * 10**9, bytes_accessed=2**20, transcendentals=0),
    )(fac, inv, left)


def halves(value):
    high = value.astype(jnp.bfloat16)
    return high, (value - high.astype(jnp.float32)).astype(jnp.bfloat16)


def inverse_rows(g_ref, g3_ref, i):
    n = BLOCK
    if i == 3:
        return g3_ref[...]
    return g_ref[i * n : (i + 1) * n, : (i + 1) * n]


def strip_kernel(at_ref, own_ref, got_ref, g_ref, g3_ref, high_ref, low_ref, z_ref, tmp):
    n = BLOCK
    for i in range(4):
        u = at_ref[0] ^ i
        tmp[i * n : (i + 1) * n, :] = jnp.where(u % 2 == 0, own_ref[u // 2], got_ref[u // 2])
    for i in range(4):
        here = slice(i * n, (i + 1) * n)
        value = dot(inverse_rows(g_ref, g3_ref, i), tmp[: (i + 1) * n, :])
        high_ref[here, :], low_ref[here, :] = halves(value)
        z_ref[here, :] = value[:, ORDER:]


def strip_solve(at, own, got, inv, inv3):
    wide = (ORDER, ORDER + BLOCK)
    return pl.pallas_call(
        strip_kernel,
        out_shape=[jax.ShapeDtypeStruct(wide, jnp.bfloat16)] * 2 + [f32(ORDER, BLOCK)],
        in_specs=[SMEM] + [VMEM] * 4,
        out_specs=[VMEM] * 3,
        scratch_shapes=[pltpu.VMEM(wide, jnp.float32)],
        compiler_params=pltpu.CompilerParams(vmem_limit_bytes=8 * 2**20),
        cost_estimate=pl.CostEstimate(flops=4 * 10**9, bytes_accessed=4 * 2**20, transcendentals=0),
    )(at, own, got, inv, inv3)


def update_kernel(at_ref, q0_ref, q1_ref, q2_ref, low_ref, high_ref, f_ref, f3_ref, g_ref, g3_ref,
                  wh_ref, wl_ref, z_ref, k_ref, y_ref, out_ref, right_ref, pan, w):
    step = pl.program_id(0)
    row, col = at_ref[2], at_ref[3]
    n = BLOCK

    def fill(read):
        for j in range(4):
            t = at_ref[1] ^ j
            for b in range(2):
                pan[b * n : (b + 1) * n, j * n : (j + 1) * n] = read(t % 2, t // 2, b)

    for s, ref in enumerate((q0_ref, q1_ref, q2_ref)):
        @pl.when(step == s)
        def _(ref=ref):
            fill(lambda t1, t2, b: ref[t1, t2, b])

    @pl.when(step == 3)
    def _():
        fill(lambda t1, t2, b: jnp.where(t1 == 0, low_ref[t2, b], high_ref[t2, b]))

    for i in range(4):
        here = slice(i * n, (i + 1) * n)
        w[:, here] = dot_nt(pan[:, : (i + 1) * n], inverse_rows(g_ref, g3_ref, i))

    first = (at_ref[4 + step] == 0) & (row < 4)

    @pl.when(first & (row < 3))
    def _():
        w[:n, :] = f_ref[pl.ds(pl.multiple_of(row * n, n), n), :]

    @pl.when(first & (row == 3))
    def _():
        w[:n, :] = f3_ref[...]

    high, low = halves(w[...])
    once = functools.partial(jnp.dot, preferred_element_type=jnp.float32)
    change = once(high, wh_ref[...]) + (once(high, wl_ref[...]) + once(low, wh_ref[...]))
    out_ref[...] = k_ref[...] - change[:, :ORDER]
    right_ref[...] = y_ref[...] - change[:, ORDER:]

    @pl.when(first)
    def _():
        out_ref[:n, :] = jnp.zeros((n, ORDER), jnp.float32)
        right_ref[:n, :] = z_ref[pl.ds(pl.multiple_of(row * n, n), n), :]

    @pl.when(col < 4)
    def _():
        out_ref[:, :n] = w[:, pl.ds(pl.multiple_of(col * n, n), n)]


def update(at, parts, factors, strips, kernel, targets):
    rows = 256
    moved = lambda width: pl.BlockSpec((rows, width), lambda s, at: (at[4 + s], 0))
    return pl.pallas_call(
        update_kernel,
        out_shape=[f32(*kernel.shape), f32(*targets.shape)],
        grid_spec=pltpu.PrefetchScalarGridSpec(
            num_scalar_prefetch=1,
            grid=(4,),
            in_specs=[VMEM] * 12 + [moved(ORDER), moved(BLOCK)],
            out_specs=[moved(ORDER), moved(BLOCK)],
            scratch_shapes=[pltpu.VMEM((rows, ORDER), jnp.float32)] * 2,
        ),
        compiler_params=pltpu.CompilerParams(vmem_limit_bytes=16 * 2**20),
        cost_estimate=pl.CostEstimate(flops=10**10, bytes_accessed=6 * 2**20, transcendentals=0),
    )(at, *parts, *factors, *strips, kernel, targets)


def after(value, *others):
    return lax.optimization_barrier((value, *others))[0]


def per_device(kernel, targets):
    row_pos = lax.axis_index("row")
    col_pos = lax.axis_index("col")
    x_pos = col_pos // Y
    y_pos = col_pos % Y
    n = BLOCK
    base = jnp.where(y_pos < 4, y_pos, 7 - y_pos)
    shifts = jnp.array([0, 3, 1, 2], jnp.int32)
    at = jnp.concatenate(
        [jnp.stack([row_pos % 4, base, row_pos, col_pos]), (x_pos + shifts) % 4]
    ).astype(jnp.int32)
    mirror = [(x * Y + j, x * Y + 7 - j) for x in range(X) for j in range(4)]
    by_two = [(c, c ^ 2) for c in range(COLS)]
    by_one = [(c, c ^ 1) for c in range(COLS)]
    by_z = [(r, r ^ 2) for r in range(ROWS)]
    by_core = [(r, r ^ 1) for r in range(ROWS)]

    a0 = jnp.where((col_pos < 4) & (row_pos < 4), kernel[:n, :n], 0.0)
    got = [a0]
    for x in (1, 2, 3):
        pairs = [(r * COLS + j, r * COLS + x * Y + j) for r in range(4) for j in range(4)]
        got.append(lax.ppermute(a0, ("row", "col"), pairs))
    a1 = total(got)

    panel = after(kernel[:, :n].reshape(8, n, n), a0)
    got = [jnp.where(x_pos == 0, panel[:2], 0.0)]
    for x in (1, 2, 3):
        got.append(over_col(panel[2 * x : 2 * x + 2], [(j, x * Y + j) for j in range(4)]))
    p1 = total(got)
    a2 = after(a1 + over_col(a1, mirror), p1)
    p2 = jnp.where(y_pos >= 4, over_col(after(p1, a1), mirror), p1)
    got = [a2]
    for a in (1, 2, 3):
        got.append(over_row(a2, [(r, r + 4 * a) for r in range(4)]))
    a3 = after(total(got), p2)

    strip = jnp.concatenate([kernel[:n], targets[:n]], axis=1)
    strip = after(jnp.where(row_pos < 4, strip, 0.0), a3)
    c1 = strip + over_row(strip, [(r, r + 12) for r in range(4)])

    a4 = jnp.stack([a3, over_col(a3, by_two)])
    a5 = after(jnp.stack([a4, over_col(a4, by_one)]), c1)
    p3 = jnp.stack([p2, over_col(after(p2, a5), by_two)])
    a6 = after(jnp.stack([a5, over_row(a5, by_z)]), p3)
    a7 = over_row(a6, by_core)
    p4_got = over_col(after(p3, a6), by_one)
    c1 = after(c1, a6)
    c2_got = over_row(c1, [(r, r + 4) for r in range(4)] + [(r, r - 4) for r in range(12, 16)])

    state = factor_first(at, a6, a7)
    p4 = jnp.stack([p3, after(p4_got, state[1])])
    c2 = c1 + after(c2_got, state[1])
    down = over_col(p4, [(c, (c + Y) % COLS) for c in range(COLS)])
    up = over_col(p4, [(c, (c - Y) % COLS) for c in range(COLS)])
    c3_got = over_row(c2, by_z)
    fac, inv, left = factor_middle(*state)
    down, up = after(down, left), after(up, left)
    c3 = jnp.stack([c2, after(c3_got, left)])
    near, far = up[0], down[1]
    low = over_col(near, [(c, (c - Y) % COLS) for c in range(COLS)])
    high = over_col(far, [(c, (c + Y) % COLS) for c in range(COLS)])
    c4 = over_row(c3, by_core)
    fac3, inv3 = factor_last(fac, inv, after(left, near, far, c3))
    strips = strip_solve(at, c3, c4, inv, inv3)
    return tuple(
        update(at, (p4, down, up, low, high), (fac, fac3, inv, inv3), strips, kernel, targets)
    )


def solution(mesh):
    in_specs = (P("row", "col"), P("row", None))
    out_specs = (P("row", "col"), P("row", None))
    return jax.shard_map(
        per_device, mesh=mesh, in_specs=in_specs, out_specs=out_specs, check_vma=False
    )
```

```python
import functools

import jax
import jax.numpy as jnp
from jax import lax
from jax.experimental import pallas as pl
from jax.experimental.pallas import tpu as pltpu
from jax.sharding import PartitionSpec as P

BLOCK = 128
ORDER = 512
X, Y = 4, 8
ROWS, COLS = 16, 32
HI = lax.Precision.HIGHEST


def over_col(value, pairs):
    return lax.ppermute(value, "col", pairs)


def over_row(value, pairs):
    return lax.ppermute(value, "row", pairs)


def dot(a, b):
    return lax.dot_general(
        a, b, (((1,), (0,)), ((), ())), precision=HI, preferred_element_type=jnp.float32
    )


def dot_nt(a, b):
    return lax.dot_general(
        a, b, (((1,), (1,)), ((), ())), precision=HI, preferred_element_type=jnp.float32
    )


def spread(value):
    return jnp.broadcast_to(value, (8, BLOCK))


def total(terms):
    terms = list(terms)
    while len(terms) > 1:
        terms = [sum(terms[i + 1 : i + 2], terms[i]) for i in range(0, len(terms), 2)]
    return terms[0]


def factor_block(s_ref, e_ref):
    ids = lax.broadcasted_iota(jnp.int32, (BLOCK, BLOCK), 0)
    lanes = lax.broadcasted_iota(jnp.int32, (BLOCK, BLOCK), 1)
    e_ref[...] = jnp.where(ids == lanes, 1.0, 0.0)
    sub = lax.broadcasted_iota(jnp.int32, (8, BLOCK), 0)
    for p in range(16):
        at = 8 * p
        own = s_ref[at : at + 8, :]
        own_e = e_ref[at : at + 8, :]
        cols = [spread(own[:, at + i : at + i + 1]) for i in range(8)]
        t = {(s, i): spread(cols[i][s : s + 1, :]) for i in range(8) for s in range(i, 8)}
        rows = [spread(own[q : q + 1, :]) for q in range(8)]
        rows_e = [spread(own_e[q : q + 1, :]) for q in range(8)]
        low, inv, root = {}, {}, []
        for i in range(8):
            rs = lax.rsqrt(t[i, i])
            root.append(rs)
            for s in range(i + 1, 8):
                low[s, i] = t[s, i] * rs
            for s in range(i + 1, 8):
                for q in range(i + 1, s + 1):
                    t[s, q] = t[s, q] - low[s, i] * low[q, i]
        for i in range(8):
            inv[i, i] = root[i]
            for s in range(i + 1, 8):
                inv[s, i] = -root[s] * total(low[s, q] * inv[q, i] for q in range(i, s))
        done = [total(inv[i, q] * rows[q] for q in range(i + 1)) for i in range(8)]
        done_e = [total(inv[i, q] * rows_e[q] for q in range(i + 1)) for i in range(8)]
        tile, tile_e = done[0], done_e[0]
        for i in range(1, 8):
            tile = jnp.where(sub == i, done[i], tile)
            tile_e = jnp.where(sub == i, done_e[i], tile_e)
        s_ref[at : at + 8, :] = tile
        e_ref[at : at + 8, :] = tile_e
        if p == 15:
            break
        back = [total(inv[i, j] * done[i] for i in range(j, 8)) for j in range(8)]
        back_e = [total(inv[i, j] * done_e[i] for i in range(j, 8)) for j in range(8)]
        for u in range(p + 1, 16):
            part = s_ref[8 * u : 8 * u + 8, :]
            left = [spread(part[:, at + j : at + j + 1]) for j in range(8)]
            s_ref[8 * u : 8 * u + 8, :] = part - total(left[j] * back[j] for j in range(8))
            e_ref[8 * u : 8 * u + 8, :] -= total(left[j] * back_e[j] for j in range(8))


def invert_block(s_ref, e_ref):
    factor_block(s_ref, e_ref)
    ids = lax.broadcasted_iota(jnp.int32, (BLOCK, BLOCK), 0)
    lanes = lax.broadcasted_iota(jnp.int32, (BLOCK, BLOCK), 1)
    return jnp.where(ids <= lanes, s_ref[...], 0.0).T, e_ref[...]


def first_kernel(at_ref, own_ref, got_ref, f_ref, g_ref, rest_ref, work, s_ref, e_ref):
    n = BLOCK
    for i in range(4):
        u = at_ref[0] ^ i
        for j in range(i + 1):
            t = at_ref[1] ^ j
            work[i * n : (i + 1) * n, j * n : (j + 1) * n] = jnp.where(
                u % 2 == 0,
                own_ref[u // 2, t % 2, t // 2],
                got_ref[u // 2, t % 2, t // 2],
            )
    s_ref[...] = work[:n, :n]
    fac, inv = invert_block(s_ref, e_ref)
    f_ref[:n, :] = fac
    g_ref[...] = inv
    f_ref[n:, :] = dot_nt(work[n:, :n], inv)
    for j in range(1, 4):
        rest_ref[(j - 1) * n :, (j - 1) * n : j * n] = work[
            j * n :, j * n : (j + 1) * n
        ] - dot_nt(f_ref[j * n :, :], f_ref[j * n : (j + 1) * n, :])


def step_kernel(k, *refs):
    n = BLOCK
    old_f, old_g, rest_ref = refs[:k], refs[k : 2 * k], refs[2 * k]
    f_ref, g_ref = refs[2 * k + 1], refs[2 * k + 2]
    s_ref, e_ref = refs[-2], refs[-1]
    s_ref[...] = rest_ref[:n, :n]
    fac, inv = invert_block(s_ref, e_ref)
    f_ref[:n, :] = fac
    g_ref[:, k * n :] = inv
    if k < 3:
        left_ref = refs[2 * k + 3]
        f_ref[n:, :] = dot_nt(rest_ref[n:, :n], inv)
        for j in range(1, 4 - k):
            left_ref[(j - 1) * n :, (j - 1) * n : j * n] = rest_ref[
                j * n :, j * n : (j + 1) * n
            ] - dot_nt(f_ref[j * n :, :], f_ref[j * n : (j + 1) * n, :])
    for j in range(k):
        here = slice(j * n, (j + 1) * n)
        part = total(
            dot(old_f[m][(k - m) * n : (k - m + 1) * n, :], old_g[m][:, here])
            for m in range(j, k)
        )
        g_ref[:, here] = -dot(inv, part)


def f32(*shape):
    return jax.ShapeDtypeStruct(shape, jnp.float32)


def b16(*shape):
    return jax.ShapeDtypeStruct(shape, jnp.bfloat16)


VMEM = pl.BlockSpec(memory_space=pltpu.VMEM)
SMEM = pl.BlockSpec(memory_space=pltpu.SMEM)
PAIR = [pltpu.VMEM((BLOCK, BLOCK), jnp.float32)] * 2
COST = pl.CostEstimate(flops=6 * 10**9, bytes_accessed=2**20, transcendentals=0)


def factor_first(at, own, got):
    return pl.pallas_call(
        first_kernel,
        out_shape=[f32(ORDER, BLOCK), f32(BLOCK, BLOCK), f32(ORDER - BLOCK, ORDER - BLOCK)],
        in_specs=[SMEM, VMEM, VMEM],
        out_specs=[VMEM] * 3,
        scratch_shapes=[pltpu.VMEM((ORDER, ORDER), jnp.float32)] + PAIR,
        compiler_params=pltpu.CompilerParams(vmem_limit_bytes=8 * 2**20),
        cost_estimate=COST,
    )(at, own, got)


def factor_step(k, fs, gs, rest):
    shapes = [f32((4 - k) * BLOCK, BLOCK), f32(BLOCK, (k + 1) * BLOCK)]
    if k < 3:
        shapes.append(f32((3 - k) * BLOCK, (3 - k) * BLOCK))
    return pl.pallas_call(
        functools.partial(step_kernel, k),
        out_shape=shapes,
        in_specs=[VMEM] * (2 * k + 1),
        out_specs=[VMEM] * len(shapes),
        scratch_shapes=PAIR,
        compiler_params=pltpu.CompilerParams(vmem_limit_bytes=8 * 2**20),
        cost_estimate=COST,
    )(*fs, *gs, rest)


def split(value, parts):
    out = []
    for _ in range(parts):
        out.append(value.astype(jnp.bfloat16))
        value = value - out[-1].astype(jnp.float32)
    return out


def once(a, b):
    return jnp.dot(a, b, preferred_element_type=jnp.float32)


def strip_kernel(at_ref, own_ref, got_ref, g0, g1, g2, g3, high_ref, low_ref, z_ref,
                 t0, t1, t2, tmp):
    n = BLOCK
    for i in range(4):
        u = at_ref[0] ^ i
        tmp[i * n : (i + 1) * n, :] = jnp.where(u % 2 == 0, own_ref[u // 2], got_ref[u // 2])
    for t_ref in (t0, t1, t2):
        t_ref[...] = jnp.zeros_like(t_ref)
    for i, g_ref in enumerate((g0, g1, g2, g3)):
        here = slice(i * n, (i + 1) * n)
        value = dot(g_ref[...], tmp[: (i + 1) * n, :])
        high_ref[here, :], low_ref[here, :] = split(value, 2)
        z_ref[here, :] = value[:, ORDER:]
        for j in range(i + 1):
            there = slice(j * n, (j + 1) * n)
            for t_ref, part in zip((t0, t1, t2), split(g_ref[:, there].T, 3)):
                t_ref[there, here] = part


def strip_solve(at, own, got, gs):
    wide = (ORDER, ORDER + BLOCK)
    return pl.pallas_call(
        strip_kernel,
        out_shape=[b16(*wide)] * 2 + [f32(ORDER, BLOCK)] + [b16(ORDER, ORDER)] * 3,
        in_specs=[SMEM] + [VMEM] * 6,
        out_specs=[VMEM] * 6,
        scratch_shapes=[pltpu.VMEM(wide, jnp.float32)],
        compiler_params=pltpu.CompilerParams(vmem_limit_bytes=8 * 2**20),
        cost_estimate=pl.CostEstimate(flops=4 * 10**9, bytes_accessed=4 * 2**20, transcendentals=0),
    )(at, own, got, *gs)


def update_kernel(at_ref, q0_ref, q1_ref, q2_ref, low_ref, high_ref, f0, f1, f2, f3,
                  wh_ref, wl_ref, z_ref, t0, t1, t2, k_ref, y_ref, out_ref, right_ref, pan, w):
    step = pl.program_id(0)
    row, col = at_ref[2], at_ref[3]
    n = BLOCK

    def fill(read):
        for j in range(4):
            t = at_ref[1] ^ j
            for b in range(2):
                pan[b * n : (b + 1) * n, j * n : (j + 1) * n] = read(t % 2, t // 2, b)

    for s, ref in enumerate((q0_ref, q1_ref, q2_ref)):
        @pl.when(step == s)
        def _(ref=ref):
            fill(lambda t1, t2, b: ref[t1, t2, b])

    @pl.when(step == 3)
    def _():
        fill(lambda t1, t2, b: jnp.where(t1 == 0, low_ref[t2, b], high_ref[t2, b]))

    p = split(pan[...], 3)
    for cols, depth in ((slice(0, 256), 256), (slice(256, 512), 512)):
        a = [part[:, :depth] for part in p]
        b = [t_ref[:depth, cols] for t_ref in (t0, t1, t2)]
        small = once(a[0], b[2]) + once(a[1], b[1]) + once(a[2], b[0])
        w[:, cols] = once(a[0], b[0]) + ((once(a[0], b[1]) + once(a[1], b[0])) + small)

    first = (at_ref[4 + step] == 0) & (row < 4)
    for i in range(4):
        @pl.when(first & (row == i))
        def _(i=i):
            w[:n, :] = jnp.zeros((n, ORDER), jnp.float32)
            for m, f_ref in enumerate((f0, f1, f2, f3)[: i + 1]):
                w[:n, m * n : (m + 1) * n] = f_ref[(i - m) * n : (i - m + 1) * n, :]

    high, low = split(w[...], 2)
    change = once(high, wh_ref[...]) + (once(high, wl_ref[...]) + once(low, wh_ref[...]))
    out_ref[...] = k_ref[...] - change[:, :ORDER]
    right_ref[...] = y_ref[...] - change[:, ORDER:]

    @pl.when(first)
    def _():
        out_ref[:n, :] = jnp.zeros((n, ORDER), jnp.float32)
        right_ref[:n, :] = z_ref[pl.ds(pl.multiple_of(row * n, n), n), :]

    @pl.when(col < 4)
    def _():
        out_ref[:, :n] = w[:, pl.ds(pl.multiple_of(col * n, n), n)]


def update(at, parts, fs, strips, kernel, targets):
    rows = 256
    moved = lambda width: pl.BlockSpec((rows, width), lambda s, at: (at[4 + s], 0))
    return pl.pallas_call(
        update_kernel,
        out_shape=[f32(*kernel.shape), f32(*targets.shape)],
        grid_spec=pltpu.PrefetchScalarGridSpec(
            num_scalar_prefetch=1,
            grid=(4,),
            in_specs=[VMEM] * 15 + [moved(ORDER), moved(BLOCK)],
            out_specs=[moved(ORDER), moved(BLOCK)],
            scratch_shapes=[pltpu.VMEM((rows, ORDER), jnp.float32)] * 2,
        ),
        compiler_params=pltpu.CompilerParams(vmem_limit_bytes=16 * 2**20),
        cost_estimate=pl.CostEstimate(flops=10**10, bytes_accessed=6 * 2**20, transcendentals=0),
    )(at, *parts, *fs, *strips, kernel, targets)


def after(value, *others):
    return lax.optimization_barrier((value, *others))[0]


def per_device(kernel, targets):
    row_pos = lax.axis_index("row")
    col_pos = lax.axis_index("col")
    x_pos = col_pos // Y
    y_pos = col_pos % Y
    n = BLOCK
    base = jnp.where(y_pos < 4, y_pos, 7 - y_pos)
    shifts = jnp.array([0, 3, 1, 2], jnp.int32)
    at = jnp.concatenate(
        [jnp.stack([row_pos % 4, base, row_pos, col_pos]), (x_pos + shifts) % 4]
    ).astype(jnp.int32)
    mirror = [(x * Y + j, x * Y + 7 - j) for x in range(X) for j in range(4)]
    by_two = [(c, c ^ 2) for c in range(COLS)]
    by_one = [(c, c ^ 1) for c in range(COLS)]
    by_z = [(r, r ^ 2) for r in range(ROWS)]
    by_core = [(r, r ^ 1) for r in range(ROWS)]

    a0 = jnp.where((col_pos < 4) & (row_pos < 4), kernel[:n, :n], 0.0)
    got = [a0]
    for x in (1, 2, 3):
        pairs = [(r * COLS + j, r * COLS + x * Y + j) for r in range(4) for j in range(4)]
        got.append(lax.ppermute(a0, ("row", "col"), pairs))
    a1 = total(got)

    pairs = [(r * COLS + a, r * COLS + b) for r in range(4) for a, b in mirror]
    a2 = a1 + lax.ppermute(a1, ("row", "col"), pairs)
    got = [a2]
    for a in (1, 2, 3):
        got.append(over_row(a2, [(r, r + 4 * a) for r in range(4)]))
    a3 = total(got)

    panel = after(kernel[:, :n].reshape(8, n, n), a2)
    got = [jnp.where(x_pos == 0, panel[:2], 0.0)]
    for x in (1, 2, 3):
        got.append(over_col(panel[2 * x : 2 * x + 2], [(j, x * Y + j) for j in range(4)]))
    p1 = total(got)
    a3 = after(a3, p1)

    strip = jnp.concatenate([kernel[:n], targets[:n]], axis=1)
    strip = after(jnp.where(row_pos < 4, strip, 0.0), a3)
    c1 = strip + over_row(strip, [(r, r + 12) for r in range(4)])

    a4 = jnp.stack([a3, over_col(a3, by_two)])
    a5 = after(jnp.stack([a4, over_col(a4, by_one)]), c1)
    p2 = jnp.where(y_pos >= 4, over_col(after(p1, a5), mirror), p1)
    a6 = after(jnp.stack([a5, over_row(a5, by_z)]), p2)
    a7 = over_row(a6, by_core)
    p2, c1 = after(p2, a6), after(c1, a6)
    p3_got = over_col(p2, by_two)
    c2_got = over_row(c1, [(r, r + 4) for r in range(4)] + [(r, r - 4) for r in range(12, 16)])

    f0, g0, rest = factor_first(at, a6, a7)
    p3 = jnp.stack([p2, after(p3_got, rest)])
    c2 = c1 + after(c2_got, rest)
    p4_got = over_col(p3, by_one)
    c3_got = over_row(c2, by_z)
    f1, g1, rest = factor_step(1, [f0], [g0], after(rest, p3, c2))
    p4 = jnp.stack([p3, after(p4_got, rest)])
    down = over_col(p4, [(c, (c + Y) % COLS) for c in range(COLS)])
    up = over_col(p4, [(c, (c - Y) % COLS) for c in range(COLS)])
    f2, g2, rest = factor_step(2, [f0, f1], [g0, g1], after(rest, p4))
    c3 = jnp.stack([c2, after(c3_got, rest)])
    c4 = over_row(c3, by_core)
    f3, g3 = factor_step(3, [f0, f1, f2], [g0, g1, g2], after(rest, c3))
    near, far = after(up, g3)[0], after(down, g3)[1]
    low = over_col(near, [(c, (c - Y) % COLS) for c in range(COLS)])
    high = over_col(far, [(c, (c + Y) % COLS) for c in range(COLS)])
    strips = strip_solve(at, c3, c4, (g0, g1, g2, after(g3, near, far)))
    return tuple(
        update(at, (p4, down, up, low, high), (f0, f1, f2, f3), strips, kernel, targets)
    )


def solution(mesh):
    in_specs = (P("row", "col"), P("row", None))
    out_specs = (P("row", "col"), P("row", None))
    return jax.shard_map(
        per_device, mesh=mesh, in_specs=in_specs, out_specs=out_specs, check_vma=False
    )
```

```python
import functools

import jax
import jax.numpy as jnp
from jax import lax
from jax.experimental import pallas as pl
from jax.experimental.pallas import tpu as pltpu
from jax.sharding import PartitionSpec as P

BLOCK = 128
ORDER = 512
X, Y = 4, 8
ROWS, COLS = 16, 32
HI = lax.Precision.HIGHEST


def over_col(value, pairs):
    return lax.ppermute(value, "col", pairs)


def over_row(value, pairs):
    return lax.ppermute(value, "row", pairs)


def dot(a, b):
    return lax.dot_general(
        a, b, (((1,), (0,)), ((), ())), precision=HI, preferred_element_type=jnp.float32
    )


def dot_nt(a, b):
    return lax.dot_general(
        a, b, (((1,), (1,)), ((), ())), precision=HI, preferred_element_type=jnp.float32
    )


def spread(value):
    return jnp.broadcast_to(value, (8, BLOCK))


def total(terms):
    terms = list(terms)
    while len(terms) > 1:
        terms = [sum(terms[i + 1 : i + 2], terms[i]) for i in range(0, len(terms), 2)]
    return terms[0]


def factor_block(s_ref, e_ref):
    ids = lax.broadcasted_iota(jnp.int32, (BLOCK, BLOCK), 0)
    lanes = lax.broadcasted_iota(jnp.int32, (BLOCK, BLOCK), 1)
    e_ref[...] = jnp.where(ids == lanes, 1.0, 0.0)
    sub = lax.broadcasted_iota(jnp.int32, (8, BLOCK), 0)
    for p in range(16):
        at = 8 * p
        own = s_ref[at : at + 8, :]
        own_e = e_ref[at : at + 8, :]
        cols = [spread(own[:, at + i : at + i + 1]) for i in range(8)]
        t = {(s, i): spread(cols[i][s : s + 1, :]) for i in range(8) for s in range(i, 8)}
        rows = [spread(own[q : q + 1, :]) for q in range(8)]
        rows_e = [spread(own_e[q : q + 1, :]) for q in range(8)]
        low, inv, root = {}, {}, []
        for i in range(8):
            rs = lax.rsqrt(t[i, i])
            root.append(rs)
            for s in range(i + 1, 8):
                low[s, i] = t[s, i] * rs
            for s in range(i + 1, 8):
                for q in range(i + 1, s + 1):
                    t[s, q] = t[s, q] - low[s, i] * low[q, i]
        for i in range(8):
            inv[i, i] = root[i]
            for s in range(i + 1, 8):
                inv[s, i] = -root[s] * total(low[s, q] * inv[q, i] for q in range(i, s))
        done = [total(inv[i, q] * rows[q] for q in range(i + 1)) for i in range(8)]
        done_e = [total(inv[i, q] * rows_e[q] for q in range(i + 1)) for i in range(8)]
        tile, tile_e = done[0], done_e[0]
        for i in range(1, 8):
            tile = jnp.where(sub == i, done[i], tile)
            tile_e = jnp.where(sub == i, done_e[i], tile_e)
        s_ref[at : at + 8, :] = tile
        e_ref[at : at + 8, :] = tile_e
        if p == 15:
            break
        back = [total(inv[i, j] * done[i] for i in range(j, 8)) for j in range(8)]
        back_e = [total(inv[i, j] * done_e[i] for i in range(j, 8)) for j in range(8)]
        for u in range(p + 1, 16):
            part = s_ref[8 * u : 8 * u + 8, :]
            left = [spread(part[:, at + j : at + j + 1]) for j in range(8)]
            s_ref[8 * u : 8 * u + 8, :] = part - total(left[j] * back[j] for j in range(8))
            e_ref[8 * u : 8 * u + 8, :] -= total(left[j] * back_e[j] for j in range(8))


def invert_block(s_ref, e_ref):
    factor_block(s_ref, e_ref)
    ids = lax.broadcasted_iota(jnp.int32, (BLOCK, BLOCK), 0)
    lanes = lax.broadcasted_iota(jnp.int32, (BLOCK, BLOCK), 1)
    return jnp.where(ids <= lanes, s_ref[...], 0.0).T, e_ref[...]


def first_kernel(at_ref, own_ref, got_ref, f_ref, g_ref, rest_ref, work, s_ref, e_ref):
    n = BLOCK
    for i in range(4):
        u = at_ref[0] ^ i
        for j in range(i + 1):
            t = at_ref[1] ^ j
            work[i * n : (i + 1) * n, j * n : (j + 1) * n] = jnp.where(
                u % 2 == 0,
                own_ref[u // 2, t % 2, t // 2],
                got_ref[u // 2, t % 2, t // 2],
            )
    s_ref[...] = work[:n, :n]
    fac, inv = invert_block(s_ref, e_ref)
    f_ref[:n, :] = fac
    g_ref[...] = inv
    f_ref[n:, :] = dot_nt(work[n:, :n], inv)
    for j in range(1, 4):
        rest_ref[(j - 1) * n :, (j - 1) * n : j * n] = work[
            j * n :, j * n : (j + 1) * n
        ] - dot_nt(f_ref[j * n :, :], f_ref[j * n : (j + 1) * n, :])


def step_kernel(k, *refs):
    n = BLOCK
    old_f, old_g, rest_ref = refs[:k], refs[k : 2 * k], refs[2 * k]
    f_ref, g_ref = refs[2 * k + 1], refs[2 * k + 2]
    s_ref, e_ref = refs[-2], refs[-1]
    s_ref[...] = rest_ref[:n, :n]
    fac, inv = invert_block(s_ref, e_ref)
    f_ref[:n, :] = fac
    g_ref[:, k * n :] = inv
    if k < 3:
        left_ref = refs[2 * k + 3]
        f_ref[n:, :] = dot_nt(rest_ref[n:, :n], inv)
        for j in range(1, 4 - k):
            left_ref[(j - 1) * n :, (j - 1) * n : j * n] = rest_ref[
                j * n :, j * n : (j + 1) * n
            ] - dot_nt(f_ref[j * n :, :], f_ref[j * n : (j + 1) * n, :])
    for j in range(k):
        here = slice(j * n, (j + 1) * n)
        part = total(
            dot(old_f[m][(k - m) * n : (k - m + 1) * n, :], old_g[m][:, here])
            for m in range(j, k)
        )
        g_ref[:, here] = -dot(inv, part)


def f32(*shape):
    return jax.ShapeDtypeStruct(shape, jnp.float32)


def b16(*shape):
    return jax.ShapeDtypeStruct(shape, jnp.bfloat16)


VMEM = pl.BlockSpec(memory_space=pltpu.VMEM)
SMEM = pl.BlockSpec(memory_space=pltpu.SMEM)
PAIR = [pltpu.VMEM((BLOCK, BLOCK), jnp.float32)] * 2
COST = pl.CostEstimate(flops=6 * 10**9, bytes_accessed=2**20, transcendentals=0)


def factor_first(at, own, got):
    return pl.pallas_call(
        first_kernel,
        out_shape=[f32(ORDER, BLOCK), f32(BLOCK, BLOCK), f32(ORDER - BLOCK, ORDER - BLOCK)],
        in_specs=[SMEM, VMEM, VMEM],
        out_specs=[VMEM] * 3,
        scratch_shapes=[pltpu.VMEM((ORDER, ORDER), jnp.float32)] + PAIR,
        compiler_params=pltpu.CompilerParams(vmem_limit_bytes=8 * 2**20),
        cost_estimate=COST,
    )(at, own, got)


def factor_step(k, fs, gs, rest):
    shapes = [f32((4 - k) * BLOCK, BLOCK), f32(BLOCK, (k + 1) * BLOCK)]
    if k < 3:
        shapes.append(f32((3 - k) * BLOCK, (3 - k) * BLOCK))
    return pl.pallas_call(
        functools.partial(step_kernel, k),
        out_shape=shapes,
        in_specs=[VMEM] * (2 * k + 1),
        out_specs=[VMEM] * len(shapes),
        scratch_shapes=PAIR,
        compiler_params=pltpu.CompilerParams(vmem_limit_bytes=8 * 2**20),
        cost_estimate=COST,
    )(*fs, *gs, rest)


def split(value, parts):
    out = []
    for _ in range(parts):
        out.append(value.astype(jnp.bfloat16))
        value = value - out[-1].astype(jnp.float32)
    return out


def once(a, b):
    return jnp.dot(a, b, preferred_element_type=jnp.float32)


def strip_kernel(at_ref, own_ref, got_ref, g0, g1, g2, g3, high_ref, low_ref, z_ref,
                 t0, t1, t2, tmp):
    n = BLOCK
    for i in range(4):
        u = at_ref[0] ^ i
        tmp[i * n : (i + 1) * n, :] = jnp.where(u % 2 == 0, own_ref[u // 2], got_ref[u // 2])
    for t_ref in (t0, t1, t2):
        t_ref[...] = jnp.zeros_like(t_ref)
    for i, g_ref in enumerate((g0, g1, g2, g3)):
        here = slice(i * n, (i + 1) * n)
        value = dot(g_ref[...], tmp[: (i + 1) * n, :])
        high_ref[here, :], low_ref[here, :] = split(value, 2)
        z_ref[here, :] = value[:, ORDER:]
        for j in range(i + 1):
            there = slice(j * n, (j + 1) * n)
            for t_ref, part in zip((t0, t1, t2), split(g_ref[:, there].T, 3)):
                t_ref[there, here] = part


def strip_solve(at, own, got, gs):
    wide = (ORDER, ORDER + BLOCK)
    return pl.pallas_call(
        strip_kernel,
        out_shape=[b16(*wide)] * 2 + [f32(ORDER, BLOCK)] + [b16(ORDER, ORDER)] * 3,
        in_specs=[SMEM] + [VMEM] * 6,
        out_specs=[VMEM] * 6,
        scratch_shapes=[pltpu.VMEM(wide, jnp.float32)],
        compiler_params=pltpu.CompilerParams(vmem_limit_bytes=8 * 2**20),
        cost_estimate=pl.CostEstimate(flops=4 * 10**9, bytes_accessed=4 * 2**20, transcendentals=0),
    )(at, own, got, *gs)


def update_kernel(at_ref, q0_ref, q1_ref, q2_ref, low_ref, high_ref, f0, f1, f2, f3,
                  wh_ref, wl_ref, z_ref, t0, t1, t2, k_ref, y_ref, out_ref, right_ref, pan, w):
    step = pl.program_id(0)
    row, col = at_ref[2], at_ref[3]
    n = BLOCK

    def fill(read):
        for j in range(4):
            t = at_ref[1] ^ j
            for b in range(2):
                pan[b * n : (b + 1) * n, j * n : (j + 1) * n] = read(t % 2, t // 2, b)

    for s, ref in enumerate((q0_ref, q1_ref, q2_ref)):
        @pl.when(step == s)
        def _(ref=ref):
            fill(lambda t1, t2, b: ref[t1, t2, b])

    @pl.when(step == 3)
    def _():
        fill(lambda t1, t2, b: jnp.where(t1 == 0, low_ref[t2, b], high_ref[t2, b]))

    p = split(pan[...], 3)
    for cols, depth in ((slice(0, 256), 256), (slice(256, 512), 512)):
        a = [part[:, :depth] for part in p]
        b = [t_ref[:depth, cols] for t_ref in (t0, t1, t2)]
        small = once(a[0], b[2]) + once(a[1], b[1]) + once(a[2], b[0])
        w[:, cols] = once(a[0], b[0]) + ((once(a[0], b[1]) + once(a[1], b[0])) + small)

    first = (at_ref[4 + step] == 0) & (row < 4)
    for i in range(4):
        @pl.when(first & (row == i))
        def _(i=i):
            w[:n, :] = jnp.zeros((n, ORDER), jnp.float32)
            for m, f_ref in enumerate((f0, f1, f2, f3)[: i + 1]):
                w[:n, m * n : (m + 1) * n] = f_ref[(i - m) * n : (i - m + 1) * n, :]

    high, low = split(w[...], 2)
    change = once(high, wh_ref[...]) + (once(high, wl_ref[...]) + once(low, wh_ref[...]))
    out_ref[...] = k_ref[...] - change[:, :ORDER]
    right_ref[...] = y_ref[...] - change[:, ORDER:]

    @pl.when(first)
    def _():
        out_ref[:n, :] = jnp.zeros((n, ORDER), jnp.float32)
        right_ref[:n, :] = z_ref[pl.ds(pl.multiple_of(row * n, n), n), :]

    @pl.when(col < 4)
    def _():
        out_ref[:, :n] = w[:, pl.ds(pl.multiple_of(col * n, n), n)]


def update(at, parts, fs, strips, kernel, targets):
    rows = 256
    moved = lambda width: pl.BlockSpec((rows, width), lambda s, at: (at[4 + s], 0))
    return pl.pallas_call(
        update_kernel,
        out_shape=[f32(*kernel.shape), f32(*targets.shape)],
        grid_spec=pltpu.PrefetchScalarGridSpec(
            num_scalar_prefetch=1,
            grid=(4,),
            in_specs=[VMEM] * 15 + [moved(ORDER), moved(BLOCK)],
            out_specs=[moved(ORDER), moved(BLOCK)],
            scratch_shapes=[pltpu.VMEM((rows, ORDER), jnp.float32)] * 2,
        ),
        compiler_params=pltpu.CompilerParams(vmem_limit_bytes=16 * 2**20),
        cost_estimate=pl.CostEstimate(flops=10**10, bytes_accessed=6 * 2**20, transcendentals=0),
    )(at, *parts, *fs, *strips, kernel, targets)


def after(value, *others):
    return lax.optimization_barrier((value, *others))[0]


def per_device(kernel, targets):
    row_pos = lax.axis_index("row")
    col_pos = lax.axis_index("col")
    x_pos = col_pos // Y
    y_pos = col_pos % Y
    n = BLOCK
    base = jnp.where(y_pos < 4, y_pos, 7 - y_pos)
    shifts = jnp.array([0, 3, 1, 2], jnp.int32)
    at = jnp.concatenate(
        [jnp.stack([row_pos % 4, base, row_pos, col_pos]), (x_pos + shifts) % 4]
    ).astype(jnp.int32)
    mirror = [(x * Y + j, x * Y + 7 - j) for x in range(X) for j in range(4)]
    by_two = [(c, c ^ 2) for c in range(COLS)]
    by_one = [(c, c ^ 1) for c in range(COLS)]
    by_z = [(r, r ^ 2) for r in range(ROWS)]
    by_core = [(r, r ^ 1) for r in range(ROWS)]

    a0 = jnp.where((col_pos < 4) & (row_pos < 4), kernel[:n, :n], 0.0)
    got = [a0]
    for x in (1, 2, 3):
        pairs = [(r * COLS + j, r * COLS + x * Y + j) for r in range(4) for j in range(4)]
        got.append(lax.ppermute(a0, ("row", "col"), pairs))
    a1 = total(got)

    pairs = [(r * COLS + a, r * COLS + b) for r in range(4) for a, b in mirror]
    a2 = a1 + lax.ppermute(a1, ("row", "col"), pairs)
    got = [a2]
    for a in (1, 2, 3):
        got.append(over_row(a2, [(r, r + 4 * a) for r in range(4)]))
    a3 = total(got)

    panel = after(kernel[:, :n].reshape(8, n, n), a2)
    got = [jnp.where(x_pos == 0, panel[:2], 0.0)]
    for x in (1, 2, 3):
        got.append(over_col(panel[2 * x : 2 * x + 2], [(j, x * Y + j) for j in range(4)]))
    p1 = total(got)
    a3 = after(a3, p1)

    a4 = jnp.stack([a3, over_col(a3, by_two)])
    p2 = jnp.where(y_pos >= 4, over_col(after(p1, a3), mirror), p1)
    a5 = after(jnp.stack([a4, over_col(a4, by_one)]), p2)
    p3 = jnp.stack([p2, over_col(after(p2, a5), by_two)])
    a6 = after(jnp.stack([a5, over_row(a5, by_z)]), p3)
    a7 = over_row(a6, by_core)
    p4_got = over_col(after(p3, a6), by_one)

    strip = jnp.concatenate([kernel[:n], targets[:n]], axis=1)
    strip = after(jnp.where(row_pos < 4, strip, 0.0), a6)
    strip_got = [over_row(strip, [(r, r + 4 * a) for r in range(4)]) for a in (1, 2, 3)]

    f0, g0, rest = factor_first(at, a6, a7)
    p4 = jnp.stack([p3, after(p4_got, rest)])
    down = over_col(p4, [(c, (c + Y) % COLS) for c in range(COLS)])
    up = over_col(p4, [(c, (c - Y) % COLS) for c in range(COLS)])
    f1, g1, rest = factor_step(1, [f0], [g0], after(rest, p4))
    f2, g2, rest = factor_step(2, [f0, f1], [g0, g1], rest)
    down, up = after(down, rest), after(up, rest)
    near, far = up[0], down[1]
    low = over_col(near, [(c, (c - Y) % COLS) for c in range(COLS)])
    high = over_col(far, [(c, (c + Y) % COLS) for c in range(COLS)])
    c2 = total([strip] + [after(got, rest) for got in strip_got])
    c3_got = over_row(c2, by_z)
    f3, g3 = factor_step(3, [f0, f1, f2], [g0, g1, g2], after(rest, near, far, c2))
    c3 = after(jnp.stack([c2, after(c3_got, g3)]), low, high)
    c4 = over_row(c3, by_core)
    strips = strip_solve(at, c3, c4, (g0, g1, g2, g3))
    return tuple(
        update(at, (p4, down, up, low, high), (f0, f1, f2, f3), strips, kernel, targets)
    )


def solution(mesh):
    in_specs = (P("row", "col"), P("row", None))
    out_specs = (P("row", "col"), P("row", None))
    return jax.shard_map(
        per_device, mesh=mesh, in_specs=in_specs, out_specs=out_specs, check_vma=False
    )
```

```python
import functools

import jax
import jax.numpy as jnp
from jax import lax
from jax.experimental import pallas as pl
from jax.experimental.pallas import tpu as pltpu
from jax.sharding import PartitionSpec as P

BLOCK = 128
ORDER = 512
X, Y = 4, 8
ROWS, COLS = 16, 32
HI = lax.Precision.HIGHEST


def over_col(value, pairs):
    return lax.ppermute(value, "col", pairs)


def over_row(value, pairs):
    return lax.ppermute(value, "row", pairs)


def dot(a, b):
    return lax.dot_general(
        a, b, (((1,), (0,)), ((), ())), precision=HI, preferred_element_type=jnp.float32
    )


def dot_nt(a, b):
    return lax.dot_general(
        a, b, (((1,), (1,)), ((), ())), precision=HI, preferred_element_type=jnp.float32
    )


def spread(value):
    return jnp.broadcast_to(value, (8, BLOCK))


def total(terms):
    terms = list(terms)
    while len(terms) > 1:
        terms = [sum(terms[i + 1 : i + 2], terms[i]) for i in range(0, len(terms), 2)]
    return terms[0]


def factor_block(s_ref, e_ref):
    ids = lax.broadcasted_iota(jnp.int32, (BLOCK, BLOCK), 0)
    lanes = lax.broadcasted_iota(jnp.int32, (BLOCK, BLOCK), 1)
    e_ref[...] = jnp.where(ids == lanes, 1.0, 0.0)
    sub = lax.broadcasted_iota(jnp.int32, (8, BLOCK), 0)
    for p in range(16):
        at = 8 * p
        own = s_ref[at : at + 8, :]
        own_e = e_ref[at : at + 8, :]
        cols = [spread(own[:, at + i : at + i + 1]) for i in range(8)]
        t = {(s, i): spread(cols[i][s : s + 1, :]) for i in range(8) for s in range(i, 8)}
        rows = [spread(own[q : q + 1, :]) for q in range(8)]
        rows_e = [spread(own_e[q : q + 1, :]) for q in range(8)]
        low, inv, root = {}, {}, []
        for i in range(8):
            rs = lax.rsqrt(t[i, i])
            root.append(rs)
            for s in range(i + 1, 8):
                low[s, i] = t[s, i] * rs
            for s in range(i + 1, 8):
                for q in range(i + 1, s + 1):
                    t[s, q] = t[s, q] - low[s, i] * low[q, i]
        for i in range(8):
            inv[i, i] = root[i]
            for s in range(i + 1, 8):
                inv[s, i] = -root[s] * total(low[s, q] * inv[q, i] for q in range(i, s))
        done = [total(inv[i, q] * rows[q] for q in range(i + 1)) for i in range(8)]
        done_e = [total(inv[i, q] * rows_e[q] for q in range(i + 1)) for i in range(8)]
        tile, tile_e = done[0], done_e[0]
        for i in range(1, 8):
            tile = jnp.where(sub == i, done[i], tile)
            tile_e = jnp.where(sub == i, done_e[i], tile_e)
        s_ref[at : at + 8, :] = tile
        e_ref[at : at + 8, :] = tile_e
        if p == 15:
            break
        back = [total(inv[i, j] * done[i] for i in range(j, 8)) for j in range(8)]
        back_e = [total(inv[i, j] * done_e[i] for i in range(j, 8)) for j in range(8)]
        for u in range(p + 1, 16):
            part = s_ref[8 * u : 8 * u + 8, :]
            left = [spread(part[:, at + j : at + j + 1]) for j in range(8)]
            s_ref[8 * u : 8 * u + 8, :] = part - total(left[j] * back[j] for j in range(8))
            e_ref[8 * u : 8 * u + 8, :] -= total(left[j] * back_e[j] for j in range(8))


def invert_block(s_ref, e_ref):
    factor_block(s_ref, e_ref)
    ids = lax.broadcasted_iota(jnp.int32, (BLOCK, BLOCK), 0)
    lanes = lax.broadcasted_iota(jnp.int32, (BLOCK, BLOCK), 1)
    return jnp.where(ids <= lanes, s_ref[...], 0.0).T, e_ref[...]


def first_kernel(at_ref, own_ref, got_ref, f_ref, g_ref, rest_ref, work, s_ref, e_ref):
    n = BLOCK
    for i in range(4):
        u = at_ref[0] ^ i
        for j in range(i + 1):
            t = at_ref[1] ^ j
            work[i * n : (i + 1) * n, j * n : (j + 1) * n] = jnp.where(
                u % 2 == 0,
                own_ref[u // 2, t % 2, t // 2],
                got_ref[u // 2, t % 2, t // 2],
            )
    s_ref[...] = work[:n, :n]
    fac, inv = invert_block(s_ref, e_ref)
    f_ref[:n, :] = fac
    g_ref[...] = inv
    f_ref[n:, :] = dot_nt(work[n:, :n], inv)
    for j in range(1, 4):
        rest_ref[(j - 1) * n :, (j - 1) * n : j * n] = work[
            j * n :, j * n : (j + 1) * n
        ] - dot_nt(f_ref[j * n :, :], f_ref[j * n : (j + 1) * n, :])


def step_kernel(k, *refs):
    n = BLOCK
    old_f, old_g, rest_ref = refs[:k], refs[k : 2 * k], refs[2 * k]
    f_ref, g_ref = refs[2 * k + 1], refs[2 * k + 2]
    s_ref, e_ref = refs[-2], refs[-1]
    s_ref[...] = rest_ref[:n, :n]
    fac, inv = invert_block(s_ref, e_ref)
    f_ref[:n, :] = fac
    g_ref[:, k * n :] = inv
    if k < 3:
        left_ref = refs[2 * k + 3]
        f_ref[n:, :] = dot_nt(rest_ref[n:, :n], inv)
        for j in range(1, 4 - k):
            left_ref[(j - 1) * n :, (j - 1) * n : j * n] = rest_ref[
                j * n :, j * n : (j + 1) * n
            ] - dot_nt(f_ref[j * n :, :], f_ref[j * n : (j + 1) * n, :])
    for j in range(k):
        here = slice(j * n, (j + 1) * n)
        part = total(
            dot(old_f[m][(k - m) * n : (k - m + 1) * n, :], old_g[m][:, here])
            for m in range(j, k)
        )
        g_ref[:, here] = -dot(inv, part)


def f32(*shape):
    return jax.ShapeDtypeStruct(shape, jnp.float32)


def b16(*shape):
    return jax.ShapeDtypeStruct(shape, jnp.bfloat16)


VMEM = pl.BlockSpec(memory_space=pltpu.VMEM)
SMEM = pl.BlockSpec(memory_space=pltpu.SMEM)
PAIR = [pltpu.VMEM((BLOCK, BLOCK), jnp.float32)] * 2
COST = pl.CostEstimate(flops=6 * 10**9, bytes_accessed=2**20, transcendentals=0)


def factor_first(at, own, got):
    return pl.pallas_call(
        first_kernel,
        out_shape=[f32(ORDER, BLOCK), f32(BLOCK, BLOCK), f32(ORDER - BLOCK, ORDER - BLOCK)],
        in_specs=[SMEM, VMEM, VMEM],
        out_specs=[VMEM] * 3,
        scratch_shapes=[pltpu.VMEM((ORDER, ORDER), jnp.float32)] + PAIR,
        compiler_params=pltpu.CompilerParams(vmem_limit_bytes=8 * 2**20),
        cost_estimate=COST,
    )(at, own, got)


def factor_step(k, fs, gs, rest):
    shapes = [f32((4 - k) * BLOCK, BLOCK), f32(BLOCK, (k + 1) * BLOCK)]
    if k < 3:
        shapes.append(f32((3 - k) * BLOCK, (3 - k) * BLOCK))
    return pl.pallas_call(
        functools.partial(step_kernel, k),
        out_shape=shapes,
        in_specs=[VMEM] * (2 * k + 1),
        out_specs=[VMEM] * len(shapes),
        scratch_shapes=PAIR,
        compiler_params=pltpu.CompilerParams(vmem_limit_bytes=8 * 2**20),
        cost_estimate=COST,
    )(*fs, *gs, rest)


def split(value, parts):
    out = []
    for _ in range(parts):
        out.append(value.astype(jnp.bfloat16))
        value = value - out[-1].astype(jnp.float32)
    return out


def once(a, b):
    return jnp.dot(a, b, preferred_element_type=jnp.float32)


def strip_kernel(at_ref, own_ref, got_ref, g0, g1, g2, g3, high_ref, low_ref, z_ref,
                 t0, t1, t2, tmp):
    n = BLOCK
    for i in range(4):
        u = at_ref[0] ^ i
        tmp[i * n : (i + 1) * n, :] = jnp.where(u % 2 == 0, own_ref[u // 2], got_ref[u // 2])
    for t_ref in (t0, t1, t2):
        t_ref[...] = jnp.zeros_like(t_ref)
    for i, g_ref in enumerate((g0, g1, g2, g3)):
        here = slice(i * n, (i + 1) * n)
        value = dot(g_ref[...], tmp[: (i + 1) * n, :])
        high_ref[here, :], low_ref[here, :] = split(value, 2)
        z_ref[here, :] = value[:, ORDER:]
        for j in range(i + 1):
            there = slice(j * n, (j + 1) * n)
            for t_ref, part in zip((t0, t1, t2), split(g_ref[:, there].T, 3)):
                t_ref[there, here] = part


def strip_solve(at, own, got, gs):
    wide = (ORDER, ORDER + BLOCK)
    return pl.pallas_call(
        strip_kernel,
        out_shape=[b16(*wide)] * 2 + [f32(ORDER, BLOCK)] + [b16(ORDER, ORDER)] * 3,
        in_specs=[SMEM] + [VMEM] * 6,
        out_specs=[VMEM] * 6,
        scratch_shapes=[pltpu.VMEM(wide, jnp.float32)],
        compiler_params=pltpu.CompilerParams(vmem_limit_bytes=8 * 2**20),
        cost_estimate=pl.CostEstimate(flops=4 * 10**9, bytes_accessed=4 * 2**20, transcendentals=0),
    )(at, own, got, *gs)


def update_kernel(at_ref, q0_ref, q1_ref, q2_ref, low_ref, high_ref, f0, f1, f2, f3,
                  wh_ref, wl_ref, z_ref, t0, t1, t2, k_ref, y_ref, out_ref, right_ref, pan, w):
    step = pl.program_id(0)
    row, col = at_ref[2], at_ref[3]
    n = BLOCK
    rows = w.shape[0]

    @pl.when(step == 0)
    def _():
        for s in range(4):
            for b in range(2):
                here = pl.ds(pl.multiple_of(at_ref[4 + s] * 2 * n + b * n, n), n)
                for j in range(4):
                    t = at_ref[1] ^ j
                    if s < 3:
                        value = (q0_ref, q1_ref, q2_ref)[s][t % 2, t // 2, b]
                    else:
                        value = jnp.where(t % 2 == 0, low_ref[t // 2, b], high_ref[t // 2, b])
                    pan[here, j * n : (j + 1) * n] = value

    p = split(pan[pl.ds(pl.multiple_of(step * rows, rows), rows), :], 3)
    for cols, depth in ((slice(0, 256), 256), (slice(256, 512), 512)):
        a = [part[:, :depth] for part in p]
        b = [t_ref[:depth, cols] for t_ref in (t0, t1, t2)]
        small = once(a[0], b[2]) + once(a[1], b[1]) + once(a[2], b[0])
        w[:, cols] = once(a[0], b[0]) + ((once(a[0], b[1]) + once(a[1], b[0])) + small)

    first = (step == 0) & (row < 4)
    for i in range(4):
        @pl.when(first & (row == i))
        def _(i=i):
            w[:n, :] = jnp.zeros((n, ORDER), jnp.float32)
            for m, f_ref in enumerate((f0, f1, f2, f3)[: i + 1]):
                w[:n, m * n : (m + 1) * n] = f_ref[(i - m) * n : (i - m + 1) * n, :]

    high, low = split(w[...], 2)
    change = once(high, wh_ref[...]) + (once(high, wl_ref[...]) + once(low, wh_ref[...]))
    out_ref[...] = k_ref[...] - change[:, :ORDER]
    right_ref[...] = y_ref[...] - change[:, ORDER:]

    @pl.when(first)
    def _():
        out_ref[:n, :] = jnp.zeros((n, ORDER), jnp.float32)
        right_ref[:n, :] = z_ref[pl.ds(pl.multiple_of(row * n, n), n), :]

    @pl.when(col < 4)
    def _():
        out_ref[:, :n] = w[:, pl.ds(pl.multiple_of(col * n, n), n)]


def update(at, parts, fs, strips, kernel, targets):
    rows = 512
    moved = lambda width: pl.BlockSpec((rows, width), lambda s: (s, 0))
    return pl.pallas_call(
        update_kernel,
        out_shape=[f32(*kernel.shape), f32(*targets.shape)],
        grid=(kernel.shape[0] // rows,),
        in_specs=[SMEM] + [VMEM] * 15 + [moved(ORDER), moved(BLOCK)],
        out_specs=[moved(ORDER), moved(BLOCK)],
        scratch_shapes=[
            pltpu.VMEM((kernel.shape[0], ORDER), jnp.float32),
            pltpu.VMEM((rows, ORDER), jnp.float32),
        ],
        compiler_params=pltpu.CompilerParams(vmem_limit_bytes=24 * 2**20),
        cost_estimate=pl.CostEstimate(flops=10**10, bytes_accessed=6 * 2**20, transcendentals=0),
    )(at, *parts, *fs, *strips, kernel, targets)


def after(value, *others):
    return lax.optimization_barrier((value, *others))[0]


def per_device(kernel, targets):
    row_pos = lax.axis_index("row")
    col_pos = lax.axis_index("col")
    x_pos = col_pos // Y
    y_pos = col_pos % Y
    n = BLOCK
    base = jnp.where(y_pos < 4, y_pos, 7 - y_pos)
    shifts = jnp.array([0, 3, 1, 2], jnp.int32)
    at = jnp.concatenate(
        [jnp.stack([row_pos % 4, base, row_pos, col_pos]), (x_pos + shifts) % 4]
    ).astype(jnp.int32)
    mirror = [(x * Y + j, x * Y + 7 - j) for x in range(X) for j in range(4)]
    by_two = [(c, c ^ 2) for c in range(COLS)]
    by_one = [(c, c ^ 1) for c in range(COLS)]
    by_z = [(r, r ^ 2) for r in range(ROWS)]
    by_core = [(r, r ^ 1) for r in range(ROWS)]

    a0 = jnp.where((col_pos < 4) & (row_pos < 4), kernel[:n, :n], 0.0)
    got = [a0]
    for x in (1, 2, 3):
        pairs = [(r * COLS + j, r * COLS + x * Y + j) for r in range(4) for j in range(4)]
        got.append(lax.ppermute(a0, ("row", "col"), pairs))
    a1 = total(got)

    pairs = [(r * COLS + a, r * COLS + b) for r in range(4) for a, b in mirror]
    a2 = a1 + lax.ppermute(a1, ("row", "col"), pairs)
    got = [a2]
    for a in (1, 2, 3):
        got.append(over_row(a2, [(r, r + 4 * a) for r in range(4)]))
    a3 = total(got)

    panel = after(kernel[:, :n].reshape(8, n, n), a2)
    got = [jnp.where(x_pos == 0, panel[:2], 0.0)]
    for x in (1, 2, 3):
        got.append(over_col(panel[2 * x : 2 * x + 2], [(j, x * Y + j) for j in range(4)]))
    p1 = total(got)
    a3 = after(a3, p1)

    a4 = jnp.stack([a3, over_col(a3, by_two)])
    p2 = jnp.where(y_pos >= 4, over_col(after(p1, a3), mirror), p1)
    a5 = after(jnp.stack([a4, over_col(a4, by_one)]), p2)
    p3 = jnp.stack([p2, over_col(after(p2, a5), by_two)])
    a6 = after(jnp.stack([a5, over_row(a5, by_z)]), p3)
    a7 = over_row(a6, by_core)
    p4_got = over_col(after(p3, a6), by_one)

    strip = jnp.concatenate([kernel[:n], targets[:n]], axis=1)
    strip = after(jnp.where(row_pos < 4, strip, 0.0), a6)
    strip_got = [over_row(strip, [(r, r + 4 * a) for r in range(4)]) for a in (1, 2, 3)]

    f0, g0, rest = factor_first(at, a6, a7)
    p4 = jnp.stack([p3, after(p4_got, rest)])
    down = over_col(p4, [(c, (c + Y) % COLS) for c in range(COLS)])
    up = over_col(p4, [(c, (c - Y) % COLS) for c in range(COLS)])
    f1, g1, rest = factor_step(1, [f0], [g0], after(rest, p4))
    c2 = total([strip] + [after(got, rest) for got in strip_got])
    c3_got = over_row(c2, by_z)
    f2, g2, rest = factor_step(2, [f0, f1], [g0, g1], after(rest, c2))
    down, up = after(down, rest), after(up, rest)
    near, far = up[0], down[1]
    low = over_col(near, [(c, (c - Y) % COLS) for c in range(COLS)])
    high = over_col(far, [(c, (c + Y) % COLS) for c in range(COLS)])
    c3 = jnp.stack([c2, after(c3_got, rest)])
    c4 = over_row(c3, by_core)
    f3, g3 = factor_step(3, [f0, f1, f2], [g0, g1, g2], after(rest, near, far, c3))
    strips = strip_solve(at, c3, after(c4, g3, low, high), (g0, g1, g2, g3))
    return tuple(
        update(at, (p4, down, up, low, high), (f0, f1, f2, f3), strips, kernel, targets)
    )


def solution(mesh):
    in_specs = (P("row", "col"), P("row", None))
    out_specs = (P("row", "col"), P("row", None))
    return jax.shard_map(
        per_device, mesh=mesh, in_specs=in_specs, out_specs=out_specs, check_vma=False
    )
```

```python
import functools

import jax
import jax.numpy as jnp
from jax import lax
from jax.experimental import pallas as pl
from jax.experimental.pallas import tpu as pltpu
from jax.sharding import PartitionSpec as P

BLOCK = 128
ORDER = 512
X, Y = 4, 8
ROWS, COLS = 16, 32
HI = lax.Precision.HIGHEST


def over_col(value, pairs):
    return lax.ppermute(value, "col", pairs)


def over_row(value, pairs):
    return lax.ppermute(value, "row", pairs)


def dot(a, b):
    return lax.dot_general(
        a, b, (((1,), (0,)), ((), ())), precision=HI, preferred_element_type=jnp.float32
    )


def dot_nt(a, b):
    return lax.dot_general(
        a, b, (((1,), (1,)), ((), ())), precision=HI, preferred_element_type=jnp.float32
    )


def spread(value):
    return jnp.broadcast_to(value, (8, BLOCK))


def total(terms):
    terms = list(terms)
    while len(terms) > 1:
        terms = [sum(terms[i + 1 : i + 2], terms[i]) for i in range(0, len(terms), 2)]
    return terms[0]


def factor_block(s_ref, e_ref):
    ids = lax.broadcasted_iota(jnp.int32, (BLOCK, BLOCK), 0)
    lanes = lax.broadcasted_iota(jnp.int32, (BLOCK, BLOCK), 1)
    e_ref[...] = jnp.where(ids == lanes, 1.0, 0.0)
    sub = lax.broadcasted_iota(jnp.int32, (8, BLOCK), 0)
    for p in range(16):
        at = 8 * p
        own = s_ref[at : at + 8, :]
        own_e = e_ref[at : at + 8, :]
        cols = [spread(own[:, at + i : at + i + 1]) for i in range(8)]
        t = {(s, i): spread(cols[i][s : s + 1, :]) for i in range(8) for s in range(i, 8)}
        rows = [spread(own[q : q + 1, :]) for q in range(8)]
        rows_e = [spread(own_e[q : q + 1, :]) for q in range(8)]
        low, inv, root = {}, {}, []
        scale = [lax.rsqrt(t[i, i]) for i in range(8)]
        for i in range(0, 8, 2):
            a = t[i, i] * (scale[i] * scale[i])
            b = t[i + 1, i] * (scale[i] * scale[i + 1])
            c = t[i + 1, i + 1] * (scale[i + 1] * scale[i + 1])
            ra = lax.rsqrt(a)
            rd = lax.rsqrt(a * c - b * b)
            one = scale[i] * ra
            two = scale[i + 1] * ((a * ra) * rd)
            root += [one, two]
            for s in range(i + 1, 8):
                low[s, i] = t[s, i] * one
            for s in range(i + 2, 8):
                low[s, i + 1] = (t[s, i + 1] - low[s, i] * low[i + 1, i]) * two
            for s in range(i + 2, 8):
                for q in range(i + 2, s + 1):
                    t[s, q] = t[s, q] - (low[s, i] * low[q, i] + low[s, i + 1] * low[q, i + 1])
        for i in range(8):
            inv[i, i] = root[i]
            for s in range(i + 1, 8):
                inv[s, i] = -root[s] * total(low[s, q] * inv[q, i] for q in range(i, s))
        done = [total(inv[i, q] * rows[q] for q in range(i + 1)) for i in range(8)]
        done_e = [total(inv[i, q] * rows_e[q] for q in range(i + 1)) for i in range(8)]
        tile, tile_e = done[0], done_e[0]
        for i in range(1, 8):
            tile = jnp.where(sub == i, done[i], tile)
            tile_e = jnp.where(sub == i, done_e[i], tile_e)
        s_ref[at : at + 8, :] = tile
        e_ref[at : at + 8, :] = tile_e
        if p == 15:
            break
        back = [total(inv[i, j] * done[i] for i in range(j, 8)) for j in range(8)]
        back_e = [total(inv[i, j] * done_e[i] for i in range(j, 8)) for j in range(8)]
        for u in range(p + 1, 16):
            part = s_ref[8 * u : 8 * u + 8, :]
            left = [spread(part[:, at + j : at + j + 1]) for j in range(8)]
            s_ref[8 * u : 8 * u + 8, :] = part - total(left[j] * back[j] for j in range(8))
            e_ref[8 * u : 8 * u + 8, :] -= total(left[j] * back_e[j] for j in range(8))


def invert_block(s_ref, e_ref):
    factor_block(s_ref, e_ref)
    ids = lax.broadcasted_iota(jnp.int32, (BLOCK, BLOCK), 0)
    lanes = lax.broadcasted_iota(jnp.int32, (BLOCK, BLOCK), 1)
    return jnp.where(ids <= lanes, s_ref[...], 0.0).T, e_ref[...]


def first_kernel(at_ref, own_ref, got_ref, f_ref, g_ref, rest_ref, work, s_ref, e_ref):
    n = BLOCK
    for i in range(4):
        u = at_ref[0] ^ i
        for j in range(i + 1):
            t = at_ref[1] ^ j
            work[i * n : (i + 1) * n, j * n : (j + 1) * n] = jnp.where(
                u % 2 == 0,
                own_ref[u // 2, t % 2, t // 2],
                got_ref[u // 2, t % 2, t // 2],
            )
    s_ref[...] = work[:n, :n]
    fac, inv = invert_block(s_ref, e_ref)
    f_ref[:n, :] = fac
    g_ref[...] = inv
    below = dot_nt(work[n:, :n], inv)
    f_ref[n:, :] = below
    rest_ref[...] = work[n:, n:] - dot_nt(below, below)


def step_kernel(k, *refs):
    n = BLOCK
    old_f, old_g, rest_ref = refs[:k], refs[k : 2 * k], refs[2 * k]
    f_ref, g_ref = refs[2 * k + 1], refs[2 * k + 2]
    sum_ref, s_ref, e_ref = refs[-3:]
    for m in reversed(range(k)):
        part = dot(old_f[m][(k - m) * n : (k - m + 1) * n, :], old_g[m][...])
        here = slice(0, (m + 1) * n)
        sum_ref[:, here] = part if m == k - 1 else sum_ref[:, here] + part
    s_ref[...] = rest_ref[:n, :n]
    fac, inv = invert_block(s_ref, e_ref)
    f_ref[:n, :] = fac
    g_ref[:, k * n :] = inv
    if k < 3:
        below = dot_nt(rest_ref[n:, :n], inv)
        f_ref[n:, :] = below
        refs[2 * k + 3][...] = rest_ref[n:, n:] - dot_nt(below, below)
    g_ref[:, : k * n] = -dot(inv, sum_ref[...])


def f32(*shape):
    return jax.ShapeDtypeStruct(shape, jnp.float32)


def b16(*shape):
    return jax.ShapeDtypeStruct(shape, jnp.bfloat16)


VMEM = pl.BlockSpec(memory_space=pltpu.VMEM)
SMEM = pl.BlockSpec(memory_space=pltpu.SMEM)
PAIR = [pltpu.VMEM((BLOCK, BLOCK), jnp.float32)] * 2
COST = pl.CostEstimate(flops=6 * 10**9, bytes_accessed=2**20, transcendentals=0)


def factor_first(at, own, got):
    return pl.pallas_call(
        first_kernel,
        out_shape=[f32(ORDER, BLOCK), f32(BLOCK, BLOCK), f32(ORDER - BLOCK, ORDER - BLOCK)],
        in_specs=[SMEM, VMEM, VMEM],
        out_specs=[VMEM] * 3,
        scratch_shapes=[pltpu.VMEM((ORDER, ORDER), jnp.float32)] + PAIR,
        compiler_params=pltpu.CompilerParams(vmem_limit_bytes=8 * 2**20),
        cost_estimate=COST,
    )(at, own, got)


def factor_step(k, fs, gs, rest):
    shapes = [f32((4 - k) * BLOCK, BLOCK), f32(BLOCK, (k + 1) * BLOCK)]
    if k < 3:
        shapes.append(f32((3 - k) * BLOCK, (3 - k) * BLOCK))
    return pl.pallas_call(
        functools.partial(step_kernel, k),
        out_shape=shapes,
        in_specs=[VMEM] * (2 * k + 1),
        out_specs=[VMEM] * len(shapes),
        scratch_shapes=[pltpu.VMEM((BLOCK, k * BLOCK), jnp.float32)] + PAIR,
        compiler_params=pltpu.CompilerParams(vmem_limit_bytes=8 * 2**20),
        cost_estimate=COST,
    )(*fs, *gs, rest)


def split(value, parts):
    out = []
    for _ in range(parts):
        out.append(value.astype(jnp.bfloat16))
        value = value - out[-1].astype(jnp.float32)
    return out


def once(a, b):
    return jnp.dot(a, b, preferred_element_type=jnp.float32)


def split_kernel(g0, g1, g2, g3, t0, t1, t2):
    n = BLOCK
    for t_ref in (t0, t1, t2):
        t_ref[...] = jnp.zeros_like(t_ref)
    for i, g_ref in enumerate((g0, g1, g2, g3)):
        here = slice(i * n, (i + 1) * n)
        for j in range(i + 1):
            there = slice(j * n, (j + 1) * n)
            for t_ref, part in zip((t0, t1, t2), split(g_ref[:, there].T, 3)):
                t_ref[there, here] = part


def split_inverse(gs):
    return pl.pallas_call(
        split_kernel,
        out_shape=[b16(ORDER, ORDER)] * 3,
        in_specs=[VMEM] * 4,
        out_specs=[VMEM] * 3,
        compiler_params=pltpu.CompilerParams(vmem_limit_bytes=8 * 2**20),
        cost_estimate=pl.CostEstimate(flops=10**9, bytes_accessed=2**21, transcendentals=0),
    )(*gs)


def strip_kernel(at_ref, own_ref, got_ref, g0, g1, g2, g3, high_ref, low_ref, z_ref, tmp):
    n = BLOCK
    for i in range(4):
        u = at_ref[0] ^ i
        tmp[i * n : (i + 1) * n, :] = jnp.where(u % 2 == 0, own_ref[u // 2], got_ref[u // 2])
    for i, g_ref in enumerate((g0, g1, g2, g3)):
        here = slice(i * n, (i + 1) * n)
        value = dot(g_ref[...], tmp[: (i + 1) * n, :])
        high_ref[here, :], low_ref[here, :] = split(value, 2)
        z_ref[here, :] = value[:, ORDER:]


def strip_solve(at, own, got, gs):
    wide = (ORDER, ORDER + BLOCK)
    return pl.pallas_call(
        strip_kernel,
        out_shape=[b16(*wide)] * 2 + [f32(ORDER, BLOCK)],
        in_specs=[SMEM] + [VMEM] * 6,
        out_specs=[VMEM] * 3,
        scratch_shapes=[pltpu.VMEM(wide, jnp.float32)],
        compiler_params=pltpu.CompilerParams(vmem_limit_bytes=8 * 2**20),
        cost_estimate=pl.CostEstimate(flops=4 * 10**9, bytes_accessed=4 * 2**20, transcendentals=0),
    )(at, own, got, *gs)


def update_kernel(at_ref, q0_ref, q1_ref, q2_ref, low_ref, high_ref, f0, f1, f2, f3,
                  wh_ref, wl_ref, z_ref, t0, t1, t2, k_ref, y_ref, out_ref, right_ref, pan, w):
    step = pl.program_id(0)
    row, col = at_ref[2], at_ref[3]
    n = BLOCK

    def fill(read):
        for j in range(4):
            t = at_ref[1] ^ j
            for b in range(2):
                pan[b * n : (b + 1) * n, j * n : (j + 1) * n] = read(t % 2, t // 2, b)

    for s, ref in enumerate((q0_ref, q1_ref, q2_ref)):
        @pl.when(step == s)
        def _(ref=ref):
            fill(lambda t1, t2, b: ref[t1, t2, b])

    @pl.when(step == 3)
    def _():
        fill(lambda t1, t2, b: jnp.where(t1 == 0, low_ref[t2, b], high_ref[t2, b]))

    p = split(pan[...], 3)
    for cols, depth in ((slice(0, 256), 256), (slice(256, 512), 512)):
        a = [part[:, :depth] for part in p]
        b = [t_ref[:depth, cols] for t_ref in (t0, t1, t2)]
        small = once(a[0], b[2]) + once(a[1], b[1]) + once(a[2], b[0])
        w[:, cols] = once(a[0], b[0]) + ((once(a[0], b[1]) + once(a[1], b[0])) + small)

    first = (at_ref[4 + step] == 0) & (row < 4)
    for i in range(4):
        @pl.when(first & (row == i))
        def _(i=i):
            w[:n, :] = jnp.zeros((n, ORDER), jnp.float32)
            for m, f_ref in enumerate((f0, f1, f2, f3)[: i + 1]):
                w[:n, m * n : (m + 1) * n] = f_ref[(i - m) * n : (i - m + 1) * n, :]

    high, low = split(w[...], 2)
    change = once(high, wh_ref[...]) + (once(high, wl_ref[...]) + once(low, wh_ref[...]))
    out_ref[...] = k_ref[...] - change[:, :ORDER]
    right_ref[...] = y_ref[...] - change[:, ORDER:]

    @pl.when(first)
    def _():
        out_ref[:n, :] = jnp.zeros((n, ORDER), jnp.float32)
        right_ref[:n, :] = z_ref[pl.ds(pl.multiple_of(row * n, n), n), :]

    @pl.when(col < 4)
    def _():
        out_ref[:, :n] = w[:, pl.ds(pl.multiple_of(col * n, n), n)]


def update(at, parts, fs, strips, kernel, targets):
    rows = 256
    moved = lambda width: pl.BlockSpec((rows, width), lambda s, at: (at[4 + s], 0))
    return pl.pallas_call(
        update_kernel,
        out_shape=[f32(*kernel.shape), f32(*targets.shape)],
        grid_spec=pltpu.PrefetchScalarGridSpec(
            num_scalar_prefetch=1,
            grid=(4,),
            in_specs=[VMEM] * 15 + [moved(ORDER), moved(BLOCK)],
            out_specs=[moved(ORDER), moved(BLOCK)],
            scratch_shapes=[pltpu.VMEM((rows, ORDER), jnp.float32)] * 2,
        ),
        compiler_params=pltpu.CompilerParams(vmem_limit_bytes=16 * 2**20),
        cost_estimate=pl.CostEstimate(flops=10**10, bytes_accessed=6 * 2**20, transcendentals=0),
    )(at, *parts, *fs, *strips, kernel, targets)


def after(value, *others):
    return lax.optimization_barrier((value, *others))[0]


def per_device(kernel, targets):
    row_pos = lax.axis_index("row")
    col_pos = lax.axis_index("col")
    x_pos = col_pos // Y
    y_pos = col_pos % Y
    n = BLOCK
    base = jnp.where(y_pos < 4, y_pos, 7 - y_pos)
    shifts = jnp.array([0, 3, 1, 2], jnp.int32)
    at = jnp.concatenate(
        [jnp.stack([row_pos % 4, base, row_pos, col_pos]), (x_pos + shifts) % 4]
    ).astype(jnp.int32)
    mirror = [(x * Y + j, x * Y + 7 - j) for x in range(X) for j in range(4)]
    by_two = [(c, c ^ 2) for c in range(COLS)]
    by_one = [(c, c ^ 1) for c in range(COLS)]
    by_z = [(r, r ^ 2) for r in range(ROWS)]
    by_core = [(r, r ^ 1) for r in range(ROWS)]

    a0 = jnp.where((col_pos < 4) & (row_pos < 4), kernel[:n, :n], 0.0)
    got = [a0]
    for x in (1, 2, 3):
        pairs = [(r * COLS + j, r * COLS + x * Y + j) for r in range(4) for j in range(4)]
        got.append(lax.ppermute(a0, ("row", "col"), pairs))
    a1 = total(got)

    pairs = [(r * COLS + a, r * COLS + b) for r in range(4) for a, b in mirror]
    a2 = a1 + lax.ppermute(a1, ("row", "col"), pairs)
    got = [a2]
    for a in (1, 2, 3):
        got.append(over_row(a2, [(r, r + 4 * a) for r in range(4)]))
    a3 = total(got)

    panel = after(kernel[:, :n].reshape(8, n, n), a2)
    got = [jnp.where(x_pos == 0, panel[:2], 0.0)]
    for x in (1, 2, 3):
        got.append(over_col(panel[2 * x : 2 * x + 2], [(j, x * Y + j) for j in range(4)]))
    p1 = total(got)
    a3 = after(a3, p1)

    a4 = jnp.stack([a3, over_col(a3, by_two)])
    p2 = jnp.where(y_pos >= 4, over_col(after(p1, a3), mirror), p1)
    a5 = after(jnp.stack([a4, over_col(a4, by_one)]), p2)
    p3 = jnp.stack([p2, over_col(after(p2, a5), by_two)])
    a6 = after(jnp.stack([a5, over_row(a5, by_z)]), p3)
    a7 = over_row(a6, by_core)
    p4_got = over_col(after(p3, a6), by_one)

    strip = jnp.concatenate([kernel[:n], targets[:n]], axis=1)
    strip = after(jnp.where(row_pos < 4, strip, 0.0), a6)
    strip_got = [over_row(strip, [(r, r + 4 * a) for r in range(4)]) for a in (1, 2, 3)]

    f0, g0, rest = factor_first(at, a6, a7)
    p4 = jnp.stack([p3, after(p4_got, rest)])
    down = over_col(p4, [(c, (c + Y) % COLS) for c in range(COLS)])
    up = over_col(p4, [(c, (c - Y) % COLS) for c in range(COLS)])
    f1, g1, rest = factor_step(1, [f0], [g0], after(rest, p4))
    f2, g2, rest = factor_step(2, [f0, f1], [g0, g1], rest)
    down, up = after(down, rest), after(up, rest)
    near, far = up[0], down[1]
    low = over_col(near, [(c, (c - Y) % COLS) for c in range(COLS)])
    high = over_col(far, [(c, (c + Y) % COLS) for c in range(COLS)])
    c2 = total([strip] + [after(got, rest) for got in strip_got])
    c3_got = over_row(c2, by_z)
    f3, g3 = factor_step(3, [f0, f1, f2], [g0, g1, g2], after(rest, near, far, c2))
    c3 = after(jnp.stack([c2, after(c3_got, g3)]), low, high)
    c4 = over_row(c3, by_core)
    parts = split_inverse((g0, g1, g2, g3))
    strips = strip_solve(at, c3, after(c4, *parts), (g0, g1, g2, g3)) + parts
    return tuple(
        update(at, (p4, down, up, low, high), (f0, f1, f2, f3), strips, kernel, targets)
    )


def solution(mesh):
    in_specs = (P("row", "col"), P("row", None))
    out_specs = (P("row", "col"), P("row", None))
    return jax.shard_map(
        per_device, mesh=mesh, in_specs=in_specs, out_specs=out_specs, check_vma=False
    )
```

```python
import functools

import jax
import jax.numpy as jnp
from jax import lax
from jax.experimental import pallas as pl
from jax.experimental.pallas import tpu as pltpu
from jax.sharding import PartitionSpec as P

BLOCK = 128
ORDER = 512
X, Y = 4, 8
ROWS, COLS = 16, 32
HI = lax.Precision.HIGHEST


def over_col(value, pairs):
    return lax.ppermute(value, "col", pairs)


def over_row(value, pairs):
    return lax.ppermute(value, "row", pairs)


def dot(a, b):
    return lax.dot_general(
        a, b, (((1,), (0,)), ((), ())), precision=HI, preferred_element_type=jnp.float32
    )


def dot_nt(a, b):
    return lax.dot_general(
        a, b, (((1,), (1,)), ((), ())), precision=HI, preferred_element_type=jnp.float32
    )


def spread(value):
    return jnp.broadcast_to(value, (8, BLOCK))


def total(terms):
    terms = list(terms)
    while len(terms) > 1:
        terms = [sum(terms[i + 1 : i + 2], terms[i]) for i in range(0, len(terms), 2)]
    return terms[0]


def factor_block(s_ref, e_ref):
    ids = lax.broadcasted_iota(jnp.int32, (BLOCK, BLOCK), 0)
    lanes = lax.broadcasted_iota(jnp.int32, (BLOCK, BLOCK), 1)
    e_ref[...] = jnp.where(ids == lanes, 1.0, 0.0)
    sub = lax.broadcasted_iota(jnp.int32, (8, BLOCK), 0)
    for p in range(16):
        at = 8 * p
        own = s_ref[at : at + 8, :]
        own_e = e_ref[at : at + 8, :]
        cols = [spread(own[:, at + i : at + i + 1]) for i in range(8)]
        t = {(s, i): spread(cols[i][s : s + 1, :]) for i in range(8) for s in range(i, 8)}
        rows = [spread(own[q : q + 1, :]) for q in range(8)]
        rows_e = [spread(own_e[q : q + 1, :]) for q in range(8)]
        low, inv, root = {}, {}, []
        scale = [lax.rsqrt(t[i, i]) for i in range(8)]
        for i in range(0, 8, 2):
            a = t[i, i] * (scale[i] * scale[i])
            b = t[i + 1, i] * (scale[i] * scale[i + 1])
            c = t[i + 1, i + 1] * (scale[i + 1] * scale[i + 1])
            ra = lax.rsqrt(a)
            rd = lax.rsqrt(a * c - b * b)
            one = scale[i] * ra
            two = scale[i + 1] * ((a * ra) * rd)
            root += [one, two]
            for s in range(i + 1, 8):
                low[s, i] = t[s, i] * one
            for s in range(i + 2, 8):
                low[s, i + 1] = (t[s, i + 1] - low[s, i] * low[i + 1, i]) * two
            for s in range(i + 2, 8):
                for q in range(i + 2, s + 1):
                    t[s, q] = t[s, q] - (low[s, i] * low[q, i] + low[s, i + 1] * low[q, i + 1])
        for i in range(8):
            inv[i, i] = root[i]
            for s in range(i + 1, 8):
                inv[s, i] = -root[s] * total(low[s, q] * inv[q, i] for q in range(i, s))
        done = [total(inv[i, q] * rows[q] for q in range(i + 1)) for i in range(8)]
        done_e = [total(inv[i, q] * rows_e[q] for q in range(i + 1)) for i in range(8)]
        tile, tile_e = done[0], done_e[0]
        for i in range(1, 8):
            tile = jnp.where(sub == i, done[i], tile)
            tile_e = jnp.where(sub == i, done_e[i], tile_e)
        s_ref[at : at + 8, :] = tile
        e_ref[at : at + 8, :] = tile_e
        if p == 15:
            break
        back = [total(inv[i, j] * done[i] for i in range(j, 8)) for j in range(8)]
        back_e = [total(inv[i, j] * done_e[i] for i in range(j, 8)) for j in range(8)]
        for u in range(p + 1, 16):
            part = s_ref[8 * u : 8 * u + 8, :]
            left = [spread(part[:, at + j : at + j + 1]) for j in range(8)]
            s_ref[8 * u : 8 * u + 8, :] = part - total(left[j] * back[j] for j in range(8))
            e_ref[8 * u : 8 * u + 8, :] -= total(left[j] * back_e[j] for j in range(8))


def invert_block(s_ref, e_ref):
    factor_block(s_ref, e_ref)
    ids = lax.broadcasted_iota(jnp.int32, (BLOCK, BLOCK), 0)
    lanes = lax.broadcasted_iota(jnp.int32, (BLOCK, BLOCK), 1)
    return jnp.where(ids <= lanes, s_ref[...], 0.0).T, e_ref[...]


def first_kernel(at_ref, own_ref, got_ref, f_ref, g_ref, rest_ref, work, s_ref, e_ref):
    n = BLOCK
    for i in range(4):
        u = at_ref[0] ^ i
        for j in range(i + 1):
            t = at_ref[1] ^ j
            work[i * n : (i + 1) * n, j * n : (j + 1) * n] = jnp.where(
                u % 2 == 0,
                own_ref[u // 2, t % 2, t // 2],
                got_ref[u // 2, t % 2, t // 2],
            )
    s_ref[...] = work[:n, :n]
    fac, inv = invert_block(s_ref, e_ref)
    f_ref[:n, :] = fac
    g_ref[...] = inv
    below = dot_nt(work[n:, :n], inv)
    f_ref[n:, :] = below
    rest_ref[...] = work[n:, n:] - dot_nt(below, below)


def step_kernel(k, *refs):
    n = BLOCK
    old_f, old_g, rest_ref = refs[:k], refs[k : 2 * k], refs[2 * k]
    f_ref, g_ref = refs[2 * k + 1], refs[2 * k + 2]
    sum_ref, s_ref, e_ref = refs[-3:]
    for m in reversed(range(k)):
        part = dot(old_f[m][(k - m) * n : (k - m + 1) * n, :], old_g[m][...])
        here = slice(0, (m + 1) * n)
        sum_ref[:, here] = part if m == k - 1 else sum_ref[:, here] + part
    s_ref[...] = rest_ref[:n, :n]
    fac, inv = invert_block(s_ref, e_ref)
    f_ref[:n, :] = fac
    g_ref[:, k * n :] = inv
    if k < 3:
        below = dot_nt(rest_ref[n:, :n], inv)
        f_ref[n:, :] = below
        refs[2 * k + 3][...] = rest_ref[n:, n:] - dot_nt(below, below)
    g_ref[:, : k * n] = -dot(inv, sum_ref[...])


def f32(*shape):
    return jax.ShapeDtypeStruct(shape, jnp.float32)


def b16(*shape):
    return jax.ShapeDtypeStruct(shape, jnp.bfloat16)


VMEM = pl.BlockSpec(memory_space=pltpu.VMEM)
SMEM = pl.BlockSpec(memory_space=pltpu.SMEM)
PAIR = [pltpu.VMEM((BLOCK, BLOCK), jnp.float32)] * 2
COST = pl.CostEstimate(flops=6 * 10**9, bytes_accessed=2**20, transcendentals=0)


def factor_first(at, own, got):
    return pl.pallas_call(
        first_kernel,
        out_shape=[f32(ORDER, BLOCK), f32(BLOCK, BLOCK), f32(ORDER - BLOCK, ORDER - BLOCK)],
        in_specs=[SMEM, VMEM, VMEM],
        out_specs=[VMEM] * 3,
        scratch_shapes=[pltpu.VMEM((ORDER, ORDER), jnp.float32)] + PAIR,
        compiler_params=pltpu.CompilerParams(vmem_limit_bytes=8 * 2**20),
        cost_estimate=COST,
    )(at, own, got)


def factor_step(k, fs, gs, rest):
    shapes = [f32((4 - k) * BLOCK, BLOCK), f32(BLOCK, (k + 1) * BLOCK)]
    if k < 3:
        shapes.append(f32((3 - k) * BLOCK, (3 - k) * BLOCK))
    return pl.pallas_call(
        functools.partial(step_kernel, k),
        out_shape=shapes,
        in_specs=[VMEM] * (2 * k + 1),
        out_specs=[VMEM] * len(shapes),
        scratch_shapes=[pltpu.VMEM((BLOCK, k * BLOCK), jnp.float32)] + PAIR,
        compiler_params=pltpu.CompilerParams(vmem_limit_bytes=8 * 2**20),
        cost_estimate=COST,
    )(*fs, *gs, rest)


def split(value, parts):
    out = []
    for _ in range(parts):
        out.append(value.astype(jnp.bfloat16))
        value = value - out[-1].astype(jnp.float32)
    return out


def once(a, b):
    return jnp.dot(a, b, preferred_element_type=jnp.float32)


def split_kernel(g0, g1, g2, g3, t0, t1, t2):
    n = BLOCK
    for t_ref in (t0, t1, t2):
        t_ref[...] = jnp.zeros_like(t_ref)
    for i, g_ref in enumerate((g0, g1, g2, g3)):
        here = slice(i * n, (i + 1) * n)
        for j in range(i + 1):
            there = slice(j * n, (j + 1) * n)
            for t_ref, part in zip((t0, t1, t2), split(g_ref[:, there].T, 3)):
                t_ref[there, here] = part


def split_inverse(gs):
    return pl.pallas_call(
        split_kernel,
        out_shape=[b16(ORDER, ORDER)] * 3,
        in_specs=[VMEM] * 4,
        out_specs=[VMEM] * 3,
        compiler_params=pltpu.CompilerParams(vmem_limit_bytes=8 * 2**20),
        cost_estimate=pl.CostEstimate(flops=10**9, bytes_accessed=2**21, transcendentals=0),
    )(*gs)


def strip_kernel(at_ref, own_ref, got_ref, g0, g1, g2, g3, high_ref, low_ref, z_ref, tmp):
    n = BLOCK
    for i in range(4):
        u = at_ref[0] ^ i
        tmp[i * n : (i + 1) * n, :] = jnp.where(u % 2 == 0, own_ref[u // 2], got_ref[u // 2])
    for i, g_ref in enumerate((g0, g1, g2, g3)):
        here = slice(i * n, (i + 1) * n)
        value = dot(g_ref[...], tmp[: (i + 1) * n, :])
        high_ref[here, :], low_ref[here, :] = split(value, 2)
        z_ref[here, :] = value[:, ORDER:]


def strip_solve(at, own, got, gs):
    wide = (ORDER, ORDER + BLOCK)
    return pl.pallas_call(
        strip_kernel,
        out_shape=[b16(*wide)] * 2 + [f32(ORDER, BLOCK)],
        in_specs=[SMEM] + [VMEM] * 6,
        out_specs=[VMEM] * 3,
        scratch_shapes=[pltpu.VMEM(wide, jnp.float32)],
        compiler_params=pltpu.CompilerParams(vmem_limit_bytes=8 * 2**20),
        cost_estimate=pl.CostEstimate(flops=4 * 10**9, bytes_accessed=4 * 2**20, transcendentals=0),
    )(at, own, got, *gs)


def update_kernel(at_ref, q0_ref, q1_ref, q2_ref, low_ref, high_ref, f0, f1, f2, f3,
                  wh_ref, wl_ref, z_ref, t0, t1, t2, k_ref, y_ref, out_ref, right_ref, pan, w):
    step = pl.program_id(0)
    row, col = at_ref[2], at_ref[3]
    n = BLOCK

    def fill(read):
        for j in range(4):
            t = at_ref[1] ^ j
            for b in range(2):
                pan[b * n : (b + 1) * n, j * n : (j + 1) * n] = read(t % 2, t // 2, b)

    for s, ref in enumerate((q0_ref, q1_ref, q2_ref)):
        @pl.when(step == s)
        def _(ref=ref):
            fill(lambda t1, t2, b: ref[t1, t2, b])

    @pl.when(step == 3)
    def _():
        fill(lambda t1, t2, b: jnp.where(t1 == 0, low_ref[t2, b], high_ref[t2, b]))

    p = split(pan[...], 3)
    for cols, depth in ((slice(0, 256), 256), (slice(256, 512), 512)):
        a = [part[:, :depth] for part in p]
        b = [t_ref[:depth, cols] for t_ref in (t0, t1, t2)]
        w[:, cols] = once(
            jnp.concatenate([a[2], a[1], a[0], a[1], a[0], a[0]], 1),
            jnp.concatenate([b[0], b[1], b[2], b[0], b[1], b[0]], 0),
        )

    first = (at_ref[4 + step] == 0) & (row < 4)
    for i in range(4):
        @pl.when(first & (row == i))
        def _(i=i):
            w[:n, :] = jnp.zeros((n, ORDER), jnp.float32)
            for m, f_ref in enumerate((f0, f1, f2, f3)[: i + 1]):
                w[:n, m * n : (m + 1) * n] = f_ref[(i - m) * n : (i - m + 1) * n, :]

    high, low = split(w[...], 2)
    change = once(
        jnp.concatenate([low, high, high], 1),
        jnp.concatenate([wh_ref[...], wl_ref[...], wh_ref[...]], 0),
    )
    out_ref[...] = k_ref[...] - change[:, :ORDER]
    right_ref[...] = y_ref[...] - change[:, ORDER:]

    @pl.when(first)
    def _():
        out_ref[:n, :] = jnp.zeros((n, ORDER), jnp.float32)
        right_ref[:n, :] = z_ref[pl.ds(pl.multiple_of(row * n, n), n), :]

    @pl.when(col < 4)
    def _():
        out_ref[:, :n] = w[:, pl.ds(pl.multiple_of(col * n, n), n)]


def update(at, parts, fs, strips, kernel, targets):
    rows = 256
    moved = lambda width: pl.BlockSpec((rows, width), lambda s, at: (at[4 + s], 0))
    return pl.pallas_call(
        update_kernel,
        out_shape=[f32(*kernel.shape), f32(*targets.shape)],
        grid_spec=pltpu.PrefetchScalarGridSpec(
            num_scalar_prefetch=1,
            grid=(4,),
            in_specs=[VMEM] * 15 + [moved(ORDER), moved(BLOCK)],
            out_specs=[moved(ORDER), moved(BLOCK)],
            scratch_shapes=[pltpu.VMEM((rows, ORDER), jnp.float32)] * 2,
        ),
        compiler_params=pltpu.CompilerParams(vmem_limit_bytes=16 * 2**20),
        cost_estimate=pl.CostEstimate(flops=10**10, bytes_accessed=6 * 2**20, transcendentals=0),
    )(at, *parts, *fs, *strips, kernel, targets)


def after(value, *others):
    return lax.optimization_barrier((value, *others))[0]


def per_device(kernel, targets):
    row_pos = lax.axis_index("row")
    col_pos = lax.axis_index("col")
    x_pos = col_pos // Y
    y_pos = col_pos % Y
    n = BLOCK
    base = jnp.where(y_pos < 4, y_pos, 7 - y_pos)
    shifts = jnp.array([0, 3, 1, 2], jnp.int32)
    at = jnp.concatenate(
        [jnp.stack([row_pos % 4, base, row_pos, col_pos]), (x_pos + shifts) % 4]
    ).astype(jnp.int32)
    mirror = [(x * Y + j, x * Y + 7 - j) for x in range(X) for j in range(4)]
    by_two = [(c, c ^ 2) for c in range(COLS)]
    by_one = [(c, c ^ 1) for c in range(COLS)]
    by_z = [(r, r ^ 2) for r in range(ROWS)]
    by_core = [(r, r ^ 1) for r in range(ROWS)]

    a0 = jnp.where((col_pos < 4) & (row_pos < 4), kernel[:n, :n], 0.0)
    got = [a0]
    for x in (1, 2, 3):
        pairs = [(r * COLS + j, r * COLS + x * Y + j) for r in range(4) for j in range(4)]
        got.append(lax.ppermute(a0, ("row", "col"), pairs))
    a1 = total(got)

    pairs = [(r * COLS + a, r * COLS + b) for r in range(4) for a, b in mirror]
    a2 = a1 + lax.ppermute(a1, ("row", "col"), pairs)
    got = [a2]
    for a in (1, 2, 3):
        got.append(over_row(a2, [(r, r + 4 * a) for r in range(4)]))
    a3 = total(got)

    panel = after(kernel[:, :n].reshape(8, n, n), a2)
    got = [jnp.where(x_pos == 0, panel[:2], 0.0)]
    for x in (1, 2, 3):
        got.append(over_col(panel[2 * x : 2 * x + 2], [(j, x * Y + j) for j in range(4)]))
    p1 = total(got)
    a3 = after(a3, p1)

    a4 = jnp.stack([a3, over_col(a3, by_two)])
    p2 = jnp.where(y_pos >= 4, over_col(after(p1, a3), mirror), p1)
    a5 = after(jnp.stack([a4, over_col(a4, by_one)]), p2)
    p3 = jnp.stack([p2, over_col(after(p2, a5), by_two)])
    a6 = after(jnp.stack([a5, over_row(a5, by_z)]), p3)
    a7 = over_row(a6, by_core)
    p4_got = over_col(after(p3, a6), by_one)

    strip = jnp.concatenate([kernel[:n], targets[:n]], axis=1)
    strip = after(jnp.where(row_pos < 4, strip, 0.0), a6)
    strip_got = [over_row(strip, [(r, r + 4 * a) for r in range(4)]) for a in (1, 2, 3)]

    f0, g0, rest = factor_first(at, a6, a7)
    p4 = jnp.stack([p3, after(p4_got, rest)])
    down = over_col(p4, [(c, (c + Y) % COLS) for c in range(COLS)])
    up = over_col(p4, [(c, (c - Y) % COLS) for c in range(COLS)])
    f1, g1, rest = factor_step(1, [f0], [g0], after(rest, p4))
    f2, g2, rest = factor_step(2, [f0, f1], [g0, g1], rest)
    down, up = after(down, rest), after(up, rest)
    near, far = up[0], down[1]
    low = over_col(near, [(c, (c - Y) % COLS) for c in range(COLS)])
    high = over_col(far, [(c, (c + Y) % COLS) for c in range(COLS)])
    c2 = total([strip] + [after(got, rest) for got in strip_got])
    c2 = after(c2, near, far)
    c3_got = over_row(c2, by_z)
    f3, g3 = factor_step(3, [f0, f1, f2], [g0, g1, g2], after(rest, near, far, c2))
    c3 = after(jnp.stack([c2, after(c3_got, g3)]), low, high)
    c4 = over_row(c3, by_core)
    parts = split_inverse((g0, g1, g2, g3))
    strips = strip_solve(at, c3, after(c4, *parts), (g0, g1, g2, g3)) + parts
    return tuple(
        update(at, (p4, down, up, low, high), (f0, f1, f2, f3), strips, kernel, targets)
    )


def solution(mesh):
    in_specs = (P("row", "col"), P("row", None))
    out_specs = (P("row", "col"), P("row", None))
    return jax.shard_map(
        per_device, mesh=mesh, in_specs=in_specs, out_specs=out_specs, check_vma=False
    )
```

```python
import functools

import jax
import jax.numpy as jnp
from jax import lax
from jax.experimental import pallas as pl
from jax.experimental.pallas import tpu as pltpu
from jax.sharding import PartitionSpec as P

BLOCK = 128
ORDER = 512
X, Y = 4, 8
ROWS, COLS = 16, 32
HI = lax.Precision.HIGHEST


def over_col(value, pairs):
    return lax.ppermute(value, "col", pairs)


def over_row(value, pairs):
    return lax.ppermute(value, "row", pairs)


def dot(a, b):
    return lax.dot_general(
        a, b, (((1,), (0,)), ((), ())), precision=HI, preferred_element_type=jnp.float32
    )


def dot_nt(a, b):
    return lax.dot_general(
        a, b, (((1,), (1,)), ((), ())), precision=HI, preferred_element_type=jnp.float32
    )


def spread(value):
    return jnp.broadcast_to(value, (8, BLOCK))


def total(terms):
    terms = list(terms)
    while len(terms) > 1:
        terms = [sum(terms[i + 1 : i + 2], terms[i]) for i in range(0, len(terms), 2)]
    return terms[0]


def factor_block(s_ref, e_ref):
    ids = lax.broadcasted_iota(jnp.int32, (BLOCK, BLOCK), 0)
    lanes = lax.broadcasted_iota(jnp.int32, (BLOCK, BLOCK), 1)
    e_ref[...] = jnp.where(ids == lanes, 1.0, 0.0)
    sub = lax.broadcasted_iota(jnp.int32, (8, BLOCK), 0)
    for p in range(16):
        at = 8 * p
        own = s_ref[at : at + 8, :]
        own_e = e_ref[at : at + 8, :]
        cols = [spread(own[:, at + i : at + i + 1]) for i in range(8)]
        t = {(s, i): spread(cols[i][s : s + 1, :]) for i in range(8) for s in range(i, 8)}
        rows = [spread(own[q : q + 1, :]) for q in range(8)]
        rows_e = [spread(own_e[q : q + 1, :]) for q in range(8)]
        low, inv, root = {}, {}, []
        scale = [lax.rsqrt(t[i, i]) for i in range(8)]
        for i in range(0, 8, 2):
            a = t[i, i] * (scale[i] * scale[i])
            b = t[i + 1, i] * (scale[i] * scale[i + 1])
            c = t[i + 1, i + 1] * (scale[i + 1] * scale[i + 1])
            ra = lax.rsqrt(a)
            rd = lax.rsqrt(a * c - b * b)
            one = scale[i] * ra
            two = scale[i + 1] * ((a * ra) * rd)
            root += [one, two]
            for s in range(i + 1, 8):
                low[s, i] = t[s, i] * one
            for s in range(i + 2, 8):
                low[s, i + 1] = (t[s, i + 1] - low[s, i] * low[i + 1, i]) * two
            for s in range(i + 2, 8):
                for q in range(i + 2, s + 1):
                    t[s, q] = t[s, q] - (low[s, i] * low[q, i] + low[s, i + 1] * low[q, i + 1])
        for i in range(8):
            inv[i, i] = root[i]
            for s in range(i + 1, 8):
                inv[s, i] = -root[s] * total(low[s, q] * inv[q, i] for q in range(i, s))
        done = [total(inv[i, q] * rows[q] for q in range(i + 1)) for i in range(8)]
        done_e = [total(inv[i, q] * rows_e[q] for q in range(i + 1)) for i in range(8)]
        tile, tile_e = done[0], done_e[0]
        for i in range(1, 8):
            tile = jnp.where(sub == i, done[i], tile)
            tile_e = jnp.where(sub == i, done_e[i], tile_e)
        s_ref[at : at + 8, :] = tile
        e_ref[at : at + 8, :] = tile_e
        if p == 15:
            break
        back = [total(inv[i, j] * done[i] for i in range(j, 8)) for j in range(8)]
        back_e = [total(inv[i, j] * done_e[i] for i in range(j, 8)) for j in range(8)]
        for u in range(p + 1, 16):
            part = s_ref[8 * u : 8 * u + 8, :]
            left = [spread(part[:, at + j : at + j + 1]) for j in range(8)]
            s_ref[8 * u : 8 * u + 8, :] = part - total(left[j] * back[j] for j in range(8))
            e_ref[8 * u : 8 * u + 8, :] -= total(left[j] * back_e[j] for j in range(8))


def invert_block(s_ref, e_ref):
    factor_block(s_ref, e_ref)
    ids = lax.broadcasted_iota(jnp.int32, (BLOCK, BLOCK), 0)
    lanes = lax.broadcasted_iota(jnp.int32, (BLOCK, BLOCK), 1)
    return jnp.where(ids <= lanes, s_ref[...], 0.0).T, e_ref[...]


def first_kernel(at_ref, own_ref, got_ref, f_ref, g_ref, rest_ref, work, s_ref, e_ref):
    n = BLOCK
    for i in range(4):
        u = at_ref[0] ^ i
        for j in range(i + 1):
            t = at_ref[1] ^ j
            work[i * n : (i + 1) * n, j * n : (j + 1) * n] = jnp.where(
                u % 2 == 0,
                own_ref[u // 2, t % 2, t // 2],
                got_ref[u // 2, t % 2, t // 2],
            )
    s_ref[...] = work[:n, :n]
    fac, inv = invert_block(s_ref, e_ref)
    f_ref[:n, :] = fac
    g_ref[...] = inv
    below = dot_nt(work[n:, :n], inv)
    f_ref[n:, :] = below
    rest_ref[...] = work[n:, n:] - dot_nt(below, below)


def step_kernel(k, *refs):
    n = BLOCK
    old_f, old_g, rest_ref = refs[:k], refs[k : 2 * k], refs[2 * k]
    f_ref, g_ref = refs[2 * k + 1], refs[2 * k + 2]
    sum_ref, s_ref, e_ref = refs[-3:]
    for m in reversed(range(k)):
        part = dot(old_f[m][(k - m) * n : (k - m + 1) * n, :], old_g[m][...])
        here = slice(0, (m + 1) * n)
        sum_ref[:, here] = part if m == k - 1 else sum_ref[:, here] + part
    s_ref[...] = rest_ref[:n, :n]
    fac, inv = invert_block(s_ref, e_ref)
    f_ref[:n, :] = fac
    g_ref[:, k * n :] = inv
    if k < 3:
        below = dot_nt(rest_ref[n:, :n], inv)
        f_ref[n:, :] = below
        refs[2 * k + 3][...] = rest_ref[n:, n:] - dot_nt(below, below)
    g_ref[:, : k * n] = -dot(inv, sum_ref[...])


def f32(*shape):
    return jax.ShapeDtypeStruct(shape, jnp.float32)


def b16(*shape):
    return jax.ShapeDtypeStruct(shape, jnp.bfloat16)


VMEM = pl.BlockSpec(memory_space=pltpu.VMEM)
SMEM = pl.BlockSpec(memory_space=pltpu.SMEM)
PAIR = [pltpu.VMEM((BLOCK, BLOCK), jnp.float32)] * 2
COST = pl.CostEstimate(flops=6 * 10**9, bytes_accessed=2**20, transcendentals=0)


def factor_first(at, own, got):
    return pl.pallas_call(
        first_kernel,
        out_shape=[f32(ORDER, BLOCK), f32(BLOCK, BLOCK), f32(ORDER - BLOCK, ORDER - BLOCK)],
        in_specs=[SMEM, VMEM, VMEM],
        out_specs=[VMEM] * 3,
        scratch_shapes=[pltpu.VMEM((ORDER, ORDER), jnp.float32)] + PAIR,
        compiler_params=pltpu.CompilerParams(vmem_limit_bytes=8 * 2**20),
        cost_estimate=COST,
    )(at, own, got)


def factor_step(k, fs, gs, rest):
    shapes = [f32((4 - k) * BLOCK, BLOCK), f32(BLOCK, (k + 1) * BLOCK)]
    if k < 3:
        shapes.append(f32((3 - k) * BLOCK, (3 - k) * BLOCK))
    return pl.pallas_call(
        functools.partial(step_kernel, k),
        out_shape=shapes,
        in_specs=[VMEM] * (2 * k + 1),
        out_specs=[VMEM] * len(shapes),
        scratch_shapes=[pltpu.VMEM((BLOCK, k * BLOCK), jnp.float32)] + PAIR,
        compiler_params=pltpu.CompilerParams(vmem_limit_bytes=8 * 2**20),
        cost_estimate=COST,
    )(*fs, *gs, rest)


def split(value, parts):
    out = []
    for _ in range(parts):
        out.append(value.astype(jnp.bfloat16))
        value = value - out[-1].astype(jnp.float32)
    return out


def once(a, b):
    return jnp.dot(a, b, preferred_element_type=jnp.float32)


def split_kernel(g0, g1, g2, g3, t0, t1, t2):
    n = BLOCK
    for t_ref in (t0, t1, t2):
        t_ref[...] = jnp.zeros_like(t_ref)
    for i, g_ref in enumerate((g0, g1, g2, g3)):
        here = slice(i * n, (i + 1) * n)
        for j in range(i + 1):
            there = slice(j * n, (j + 1) * n)
            for t_ref, part in zip((t0, t1, t2), split(g_ref[:, there].T, 3)):
                t_ref[there, here] = part


def split_inverse(gs):
    return pl.pallas_call(
        split_kernel,
        out_shape=[b16(ORDER, ORDER)] * 3,
        in_specs=[VMEM] * 4,
        out_specs=[VMEM] * 3,
        compiler_params=pltpu.CompilerParams(vmem_limit_bytes=8 * 2**20),
        cost_estimate=pl.CostEstimate(flops=10**9, bytes_accessed=2**21, transcendentals=0),
    )(*gs)


def strip_kernel(at_ref, own_ref, got_ref, g0, g1, g2, g3, high_ref, low_ref, z_ref, tmp):
    n = BLOCK
    for i in range(4):
        u = at_ref[0] ^ i
        tmp[i * n : (i + 1) * n, :] = jnp.where(u % 2 == 0, own_ref[u // 2], got_ref[u // 2])
    top = split(tmp[...], 3)
    for i, g_ref in enumerate((g0, g1, g2, g3)):
        here = slice(i * n, (i + 1) * n)
        a = split(g_ref[...], 3)
        b = [part[: (i + 1) * n, :] for part in top]
        value = once(
            jnp.concatenate([a[2], a[1], a[0], a[1], a[0], a[0]], 1),
            jnp.concatenate([b[0], b[1], b[2], b[0], b[1], b[0]], 0),
        )
        high_ref[here, :], low_ref[here, :] = split(value, 2)
        z_ref[here, :] = value[:, ORDER:]


def strip_solve(at, own, got, gs):
    wide = (ORDER, ORDER + BLOCK)
    return pl.pallas_call(
        strip_kernel,
        out_shape=[b16(*wide)] * 2 + [f32(ORDER, BLOCK)],
        in_specs=[SMEM] + [VMEM] * 6,
        out_specs=[VMEM] * 3,
        scratch_shapes=[pltpu.VMEM(wide, jnp.float32)],
        compiler_params=pltpu.CompilerParams(vmem_limit_bytes=8 * 2**20),
        cost_estimate=pl.CostEstimate(flops=4 * 10**9, bytes_accessed=4 * 2**20, transcendentals=0),
    )(at, own, got, *gs)


def update_kernel(at_ref, q0_ref, q1_ref, q2_ref, low_ref, high_ref, f0, f1, f2, f3,
                  wh_ref, wl_ref, z_ref, t0, t1, t2, k_ref, y_ref, out_ref, right_ref, pan, w):
    step = pl.program_id(0)
    row, col = at_ref[2], at_ref[3]
    n = BLOCK

    def fill(read):
        for j in range(4):
            t = at_ref[1] ^ j
            for b in range(2):
                pan[b * n : (b + 1) * n, j * n : (j + 1) * n] = read(t % 2, t // 2, b)

    for s, ref in enumerate((q0_ref, q1_ref, q2_ref)):
        @pl.when(step == s)
        def _(ref=ref):
            fill(lambda t1, t2, b: ref[t1, t2, b])

    @pl.when(step == 3)
    def _():
        fill(lambda t1, t2, b: jnp.where(t1 == 0, low_ref[t2, b], high_ref[t2, b]))

    p = split(pan[...], 3)
    for cols, depth in ((slice(0, 256), 256), (slice(256, 512), 512)):
        a = [part[:, :depth] for part in p]
        b = [t_ref[:depth, cols] for t_ref in (t0, t1, t2)]
        w[:, cols] = once(
            jnp.concatenate([a[2], a[1], a[0], a[1], a[0], a[0]], 1),
            jnp.concatenate([b[0], b[1], b[2], b[0], b[1], b[0]], 0),
        )

    first = (at_ref[4 + step] == 0) & (row < 4)
    for i in range(4):
        @pl.when(first & (row == i))
        def _(i=i):
            w[:n, :] = jnp.zeros((n, ORDER), jnp.float32)
            for m, f_ref in enumerate((f0, f1, f2, f3)[: i + 1]):
                w[:n, m * n : (m + 1) * n] = f_ref[(i - m) * n : (i - m + 1) * n, :]

    high, low = split(w[...], 2)
    change = once(
        jnp.concatenate([low, high, high], 1),
        jnp.concatenate([wh_ref[...], wl_ref[...], wh_ref[...]], 0),
    )
    out_ref[...] = k_ref[...] - change[:, :ORDER]
    right_ref[...] = y_ref[...] - change[:, ORDER:]

    @pl.when(first)
    def _():
        out_ref[:n, :] = jnp.zeros((n, ORDER), jnp.float32)
        right_ref[:n, :] = z_ref[pl.ds(pl.multiple_of(row * n, n), n), :]

    @pl.when(col < 4)
    def _():
        out_ref[:, :n] = w[:, pl.ds(pl.multiple_of(col * n, n), n)]


def update(at, parts, fs, strips, kernel, targets):
    rows = 256
    moved = lambda width: pl.BlockSpec((rows, width), lambda s, at: (at[4 + s], 0))
    return pl.pallas_call(
        update_kernel,
        out_shape=[f32(*kernel.shape), f32(*targets.shape)],
        grid_spec=pltpu.PrefetchScalarGridSpec(
            num_scalar_prefetch=1,
            grid=(4,),
            in_specs=[VMEM] * 15 + [moved(ORDER), moved(BLOCK)],
            out_specs=[moved(ORDER), moved(BLOCK)],
            scratch_shapes=[pltpu.VMEM((rows, ORDER), jnp.float32)] * 2,
        ),
        compiler_params=pltpu.CompilerParams(vmem_limit_bytes=16 * 2**20),
        cost_estimate=pl.CostEstimate(flops=10**10, bytes_accessed=6 * 2**20, transcendentals=0),
    )(at, *parts, *fs, *strips, kernel, targets)


def after(value, *others):
    return lax.optimization_barrier((value, *others))[0]


def per_device(kernel, targets):
    row_pos = lax.axis_index("row")
    col_pos = lax.axis_index("col")
    x_pos = col_pos // Y
    y_pos = col_pos % Y
    n = BLOCK
    base = jnp.where(y_pos < 4, y_pos, 7 - y_pos)
    shifts = jnp.array([0, 3, 1, 2], jnp.int32)
    at = jnp.concatenate(
        [jnp.stack([row_pos % 4, base, row_pos, col_pos]), (x_pos + shifts) % 4]
    ).astype(jnp.int32)
    mirror = [(x * Y + j, x * Y + 7 - j) for x in range(X) for j in range(4)]
    by_two = [(c, c ^ 2) for c in range(COLS)]
    by_one = [(c, c ^ 1) for c in range(COLS)]
    by_z = [(r, r ^ 2) for r in range(ROWS)]
    by_core = [(r, r ^ 1) for r in range(ROWS)]

    a0 = jnp.where((col_pos < 4) & (row_pos < 4), kernel[:n, :n], 0.0)
    got = [a0]
    for x in (1, 2, 3):
        pairs = [(r * COLS + j, r * COLS + x * Y + j) for r in range(4) for j in range(4)]
        got.append(lax.ppermute(a0, ("row", "col"), pairs))
    a1 = total(got)

    pairs = [(r * COLS + a, r * COLS + b) for r in range(4) for a, b in mirror]
    a2 = a1 + lax.ppermute(a1, ("row", "col"), pairs)
    got = [a2]
    for a in (1, 2, 3):
        got.append(over_row(a2, [(r, r + 4 * a) for r in range(4)]))
    a3 = total(got)

    panel = after(kernel[:, :n].reshape(8, n, n), a2)
    got = [jnp.where(x_pos == 0, panel[:2], 0.0)]
    for x in (1, 2, 3):
        got.append(over_col(panel[2 * x : 2 * x + 2], [(j, x * Y + j) for j in range(4)]))
    p1 = total(got)
    a3 = after(a3, p1)

    a4 = jnp.stack([a3, over_col(a3, by_two)])
    p2 = jnp.where(y_pos >= 4, over_col(after(p1, a3), mirror), p1)
    a5 = after(jnp.stack([a4, over_col(a4, by_one)]), p2)
    p3 = jnp.stack([p2, over_col(after(p2, a5), by_two)])
    a6 = after(jnp.stack([a5, over_row(a5, by_z)]), p3)
    a7 = over_row(a6, by_core)
    p4_got = over_col(after(p3, a6), by_one)

    strip = jnp.concatenate([kernel[:n], targets[:n]], axis=1)
    strip = after(jnp.where(row_pos < 4, strip, 0.0), a6)
    strip_got = [over_row(strip, [(r, r + 4 * a) for r in range(4)]) for a in (1, 2, 3)]

    f0, g0, rest = factor_first(at, a6, a7)
    p4 = jnp.stack([p3, after(p4_got, rest)])
    down = over_col(p4, [(c, (c + Y) % COLS) for c in range(COLS)])
    up = over_col(p4, [(c, (c - Y) % COLS) for c in range(COLS)])
    f1, g1, rest = factor_step(1, [f0], [g0], after(rest, p4))
    f2, g2, rest = factor_step(2, [f0, f1], [g0, g1], rest)
    down, up = after(down, rest), after(up, rest)
    near, far = up[0], down[1]
    low = over_col(near, [(c, (c - Y) % COLS) for c in range(COLS)])
    high = over_col(far, [(c, (c + Y) % COLS) for c in range(COLS)])
    c2 = total([strip] + [after(got, rest) for got in strip_got])
    c2 = after(c2, near, far)
    c3_got = over_row(c2, by_z)
    f3, g3 = factor_step(3, [f0, f1, f2], [g0, g1, g2], after(rest, near, far, c2))
    c3 = after(jnp.stack([c2, after(c3_got, g3)]), low, high)
    c4 = over_row(c3, by_core)
    parts = split_inverse((g0, g1, g2, g3))
    strips = strip_solve(at, c3, after(c4, *parts), (g0, g1, g2, g3)) + parts
    return tuple(
        update(at, (p4, down, up, low, high), (f0, f1, f2, f3), strips, kernel, targets)
    )


def solution(mesh):
    in_specs = (P("row", "col"), P("row", None))
    out_specs = (P("row", "col"), P("row", None))
    return jax.shard_map(
        per_device, mesh=mesh, in_specs=in_specs, out_specs=out_specs, check_vma=False
    )
```
